512 devices in a mesh: tm: 64 (over z_lo, y, x), tile: 8 (over z_hi, core).
Axes of the slice: x: 4, y: 8, z: 8 (z_hi: 4, z_lo: 2; z = z_hi * 2 + z_lo), core: 2. Of those that a mesh axis runs over, the one named last changes fastest.
Arguments:
- latent: bfloat16 [256, 32, 160, 128], P('tm', 'tile'), may hold values from -6 to 6
- cot_forward: bfloat16 [256, 32, 160, 128], P('tm', 'tile'), may hold values from -6 to 6
- cot_reverse: bfloat16 [256, 32, 160, 128], P('tm', 'tile'), may hold values from -6 to 6
- spatial_weight: bfloat16 [3, 3, 128, 128], replicated, may hold values from -0.1875 to 0.1875
- temporal_weight: bfloat16 [3, 128, 128], replicated, may hold values from -0.3125 to 0.3125
Outputs:
- out_forward: bfloat16 [256, 32, 160, 128], P('tm', 'tile')
- out_reverse: bfloat16 [256, 32, 160, 128], P('tm', 'tile')
- grad_input: bfloat16 [256, 32, 160, 128], P('tm', 'tile')
- grad_spatial: float32 [3, 3, 128, 128], replicated
- grad_temporal: float32 [3, 128, 128], replicated
The draws below stay inside these ranges and needn't reach their ends.
All inputs are finite; a program needn't handle non-finite values.
Results may differ from the reference program's by a relative error of at most 0.0032.
Values may be sent and summed in bfloat16 or wider, within the bound.
No kernel may reach another device: no remote copies, remote signals or barrier semaphores. Data moves between devices by JAX's collectives and lax.ppermute only.
A program may use at most 64 MiB of HBM per device.

```python
import math
import jax
import jax.numpy as jnp
from jax import lax

C = 128
W = 160
FRAMES = 256
ROWS = 32


def levels(key, extent, pieces, least, largest):
    factor_of, own = 1.0, jax.random.fold_in(key, 6)
    for axis_at, blocks in pieces:
        steps = jnp.exp(jax.random.uniform(jax.random.fold_in(own, axis_at), (blocks,), jnp.float32, least / len(pieces), largest / len(pieces)))
        factor_of = factor_of * jnp.repeat(steps, extent[axis_at] // blocks).reshape([-1 if axis == axis_at else 1 for axis in range(len(extent))])
    return factor_of


def noise(stream_key, extent, spread, reach, pieces=(), kind=jnp.bfloat16):
    drawn = jax.random.normal(stream_key, extent, jnp.float32) * spread
    if len(pieces) > 0:
        drawn = levels(stream_key, extent, pieces, -0.22, 0.18) * drawn
    return jnp.clip(drawn, min=-reach, max=reach).astype(kind)


def setup_inputs(seed: int = 0) -> dict:
    splits = jax.random.split(jax.random.key(seed), 6)
    latent = noise(splits[0], (FRAMES, ROWS, W, C), 1.0, 6.0, ((0, 64), (1, 8)))
    cot_forward = noise(splits[1], (FRAMES, ROWS, W, C), 1.0, 6.0, ((0, 64), (1, 8)))
    cot_reverse = noise(splits[2], (FRAMES, ROWS, W, C), 1.0, 6.0, ((0, 64), (1, 8)))
    spatial_weight = noise(splits[3], (3, 3, C, C), (9 * C) ** -0.5, 0.1875)
    temporal_weight = noise(splits[4], (3, C, C), (3 * C) ** -0.5, 0.3125)
    return {"latent": latent, "cot_forward": cot_forward, "cot_reverse": cot_reverse, "spatial_weight": spatial_weight, "temporal_weight": temporal_weight}


def flat(values):
    return values.reshape(-1, values.shape[-1])

def shift_frames(values, lag_steps):
    if lag_steps > 0:
        return jnp.concatenate([jnp.zeros_like(values[:lag_steps]), values[:-lag_steps]], axis=0)
    if lag_steps < 0:
        return jnp.concatenate([values[-lag_steps:], jnp.zeros_like(values[:-lag_steps])], axis=0)
    return values

def contract_rows(left, right):
    return lax.dot_general(left, right, (((0,), (0,)), ((), ())), preferred_element_type=jnp.float32)

def reference(latent, cot_forward, cot_reverse, spatial_weight, temporal_weight):
    frame_count, height, width_cells, channels = latent.shape
    padded = jnp.pad(latent, ((0, 0), (1, 1), (1, 1), (0, 0)))
    pre_act = jnp.zeros((frame_count * height * width_cells, channels), jnp.float32)
    for row_step in range(3):
        for col_step in range(3):
            window = flat(padded[:, row_step:row_step + height, col_step:col_step + width_cells, :])
            pre_act = pre_act + jnp.dot(window, spatial_weight[row_step, col_step], preferred_element_type=jnp.float32)
    act = jax.nn.silu(pre_act).astype(jnp.bfloat16).reshape(latent.shape)

    def causal_out(source_latent, source_act):
        total = flat(source_latent).astype(jnp.float32)
        for lag_steps in range(3):
            total = total + jnp.dot(flat(shift_frames(source_act, lag_steps)), temporal_weight[lag_steps], preferred_element_type=jnp.float32)
        return total.astype(jnp.bfloat16).reshape(latent.shape)
    out_forward = causal_out(latent, act)
    out_reverse = causal_out(latent[::-1], act[::-1])[::-1]
    grad_act = jnp.zeros((frame_count * height * width_cells, channels), jnp.float32)
    grad_temp = []
    for lag_steps in range(3):
        weight_back = jnp.transpose(temporal_weight[lag_steps])
        grad_act = grad_act + jnp.dot(flat(shift_frames(cot_forward, -lag_steps)), weight_back, preferred_element_type=jnp.float32)
        grad_act = grad_act + jnp.dot(flat(shift_frames(cot_reverse, lag_steps)), weight_back, preferred_element_type=jnp.float32)
        term = contract_rows(flat(shift_frames(act, lag_steps)), flat(cot_forward))
        term = term + contract_rows(flat(shift_frames(act, -lag_steps)), flat(cot_reverse))
        grad_temp.append(term)
    sigmoid_pre = jax.nn.sigmoid(pre_act)
    grad_pre = (grad_act * sigmoid_pre * (1.0 + pre_act * (1.0 - sigmoid_pre))).astype(jnp.bfloat16)
    grad_padded = jnp.pad(grad_pre.reshape(latent.shape), ((0, 0), (1, 1), (1, 1), (0, 0)))
    total_in = flat(cot_forward).astype(jnp.float32) + flat(cot_reverse).astype(jnp.float32)
    grad_space = []
    for row_step in range(3):
        for col_step in range(3):
            window = flat(grad_padded[:, 2 - row_step:2 - row_step + height, 2 - col_step:2 - col_step + width_cells, :])
            total_in = total_in + jnp.dot(window, jnp.transpose(spatial_weight[row_step, col_step]), preferred_element_type=jnp.float32)
            source = flat(padded[:, row_step:row_step + height, col_step:col_step + width_cells, :])
            grad_space.append(contract_rows(source, grad_pre))
    grad_input = total_in.astype(jnp.bfloat16).reshape(latent.shape)
    grad_scale = 1.0 / math.sqrt(frame_count * height * width_cells)
    grad_spatial = jnp.stack(grad_space).reshape(3, 3, channels, channels) * grad_scale
    grad_temporal = jnp.stack(grad_temp) * grad_scale
    return (out_forward, out_reverse, grad_input, grad_spatial, grad_temporal)
```

```python
import math

import jax
import jax.numpy as jnp
from jax import lax
from jax.sharding import PartitionSpec as P

BOTH = ("tm", "tile")


def groups(bits):
    rest = [b for b in range(9) if b not in bits]
    out = []
    for r in range(1 << len(rest)):
        base = sum(((r >> i) & 1) << b for i, b in enumerate(rest))
        members = []
        for k in range(1 << len(bits)):
            members.append(base + sum(((k >> i) & 1) << b for i, b in enumerate(reversed(bits))))
        out.append(members)
    return out


NEAR = groups([8, 5, 4, 3, 0])
FAR = groups([7, 6, 2, 1])


def exchange(pieces, members):
    return lax.all_to_all(pieces, BOTH, 0, 0, tiled=True, axis_index_groups=members)


def to_all(shard, members):
    return exchange(jnp.broadcast_to(shard[None], (len(members[0]), *shard.shape)), members)


def total_over_mesh(partial):
    rows, channels = partial.shape
    near = len(NEAR[0])
    pieces = partial.astype(jnp.bfloat16).reshape(near, rows // near, channels)
    share = exchange(pieces, NEAR).astype(jnp.float32).sum(axis=0)
    share = to_all(share.astype(jnp.bfloat16), FAR).astype(jnp.float32).sum(axis=0)
    whole = to_all(share.astype(jnp.bfloat16), NEAR)
    return whole.reshape(rows, channels).astype(jnp.float32)


def shifted(value, axis, steps):
    count = lax.axis_size(axis)
    initial, last = (max(0, -steps), min(count, count - steps))
    return lax.ppermute(value, axis, [(source, source + steps) for source in range(initial, last)])


def rim(cells, axis, dim, width):
    head = lax.slice_in_dim(cells, 0, width, axis=dim)
    tail = lax.slice_in_dim(cells, cells.shape[dim] - width, cells.shape[dim], axis=dim)
    return jnp.concatenate([shifted(tail, axis, 1), cells, shifted(head, axis, -1)], axis=dim)


def spatial_rows(padded, height, width_cells, flipped):
    pieces = []
    for row_step in range(3):
        for col_step in range(3):
            row_from = 2 - row_step if flipped else row_step
            col_from = 2 - col_step if flipped else col_step
            pieces.append(
                padded[:, row_from : row_from + height, col_from : col_from + width_cells, :]
            )
    joined = jnp.concatenate(pieces, axis=3)
    return joined.reshape(-1, joined.shape[3])


def widen(values):
    return jnp.pad(values, ((0, 0), (0, 0), (1, 1), (0, 0)))


def temporal_rows(extended, offsets, frame_count):
    joined = jnp.concatenate(
        [extended[offset : offset + frame_count] for offset in offsets], axis=2
    )
    return joined.reshape(-1, joined.shape[2])


def contract_rows(left, right):
    return lax.dot_general(
        left, right, (((0,), (0,)), ((), ())), preferred_element_type=jnp.float32
    )


def body(latent, cot_forward, cot_reverse, spatial_weight, temporal_weight):
    frame_count, height, width_cells, channels = latent.shape
    plane_cells = height * width_cells
    spatial_flat = spatial_weight.reshape(9 * channels, channels)
    flipped_flat = jnp.transpose(spatial_weight, (0, 1, 3, 2)).reshape(9 * channels, channels)
    forward_flat = temporal_weight.reshape(3 * channels, channels)
    backward_flat = jnp.transpose(temporal_weight, (0, 2, 1)).reshape(3 * channels, channels)
    latent_flat = latent.reshape(-1, channels)
    fwd_cot = cot_forward.reshape(frame_count, plane_cells, channels)
    rev_cot = cot_reverse.reshape(frame_count, plane_cells, channels)
    following = shifted(fwd_cot[:2], "tm", -1)
    earlier = shifted(rev_cot[-2:], "tm", 1)
    rimmed = rim(latent, "tile", 1, 1)
    patches = spatial_rows(widen(rimmed), height, width_cells, False)
    pre_act = jnp.dot(patches, spatial_flat, preferred_element_type=jnp.float32)
    act_flat = jax.nn.silu(pre_act).astype(jnp.bfloat16)
    act_frames = act_flat.reshape(frame_count, plane_cells, channels)
    ahead = temporal_rows(jnp.concatenate([fwd_cot, following], axis=0), (0, 1, 2), frame_count)
    behind = temporal_rows(jnp.concatenate([earlier, rev_cot], axis=0), (2, 1, 0), frame_count)
    grad_act = jnp.dot(ahead, backward_flat, preferred_element_type=jnp.float32)
    grad_act = grad_act + jnp.dot(behind, backward_flat, preferred_element_type=jnp.float32)
    grad_temp = contract_rows(ahead, act_flat) + contract_rows(behind, act_flat)
    grad_temp = jnp.transpose(grad_temp.reshape(3, channels, channels), (0, 2, 1))
    sigmoid_pre = jax.nn.sigmoid(pre_act)
    grad_pre = (grad_act * sigmoid_pre * (1.0 + pre_act * (1.0 - sigmoid_pre))).astype(jnp.bfloat16)
    grad_space = contract_rows(patches, grad_pre)
    partial = jnp.concatenate([grad_space, grad_temp.reshape(3 * channels, channels)], axis=0)
    whole = total_over_mesh(partial)

    rimmed_act = rim(act_frames, "tm", 0, 2)
    causal = temporal_rows(rimmed_act, (2, 1, 0), frame_count)
    anticausal = temporal_rows(rimmed_act, (2, 3, 4), frame_count)
    residual_in = latent_flat.astype(jnp.float32)
    out_forward = (
        (residual_in + jnp.dot(causal, forward_flat, preferred_element_type=jnp.float32))
        .astype(jnp.bfloat16)
        .reshape(latent.shape)
    )
    out_reverse = (
        (residual_in + jnp.dot(anticausal, forward_flat, preferred_element_type=jnp.float32))
        .astype(jnp.bfloat16)
        .reshape(latent.shape)
    )
    grad_rim = rim(grad_pre.reshape(latent.shape), "tile", 1, 1)
    grad_patches = spatial_rows(widen(grad_rim), height, width_cells, True)
    total_in = cot_forward.reshape(-1, channels).astype(jnp.float32) + cot_reverse.reshape(
        -1, channels
    ).astype(jnp.float32)
    total_in = total_in + jnp.dot(grad_patches, flipped_flat, preferred_element_type=jnp.float32)
    grad_input = total_in.astype(jnp.bfloat16).reshape(latent.shape)
    positions = frame_count * height * width_cells * lax.axis_size("tm") * lax.axis_size("tile")
    whole = whole * (1.0 / math.sqrt(positions))
    grad_spatial = whole[: 9 * channels].reshape(3, 3, channels, channels)
    grad_temporal = whole[9 * channels :].reshape(3, channels, channels)
    return (out_forward, out_reverse, grad_input, grad_spatial, grad_temporal)


def solution(mesh):
    cells = P("tm", "tile", None, None)
    return jax.shard_map(
        body,
        mesh=mesh,
        in_specs=(cells, cells, cells, P(), P()),
        out_specs=(cells, cells, cells, P(), P()),
        check_vma=False,
    )
```

```python
import functools
import math

import jax
import jax.numpy as jnp
from jax import lax
from jax.experimental import pallas as pl
from jax.experimental.pallas import tpu as pltpu
from jax.sharding import PartitionSpec as P

BOTH = ("tm", "tile")
F32 = jnp.float32
BF16 = jnp.bfloat16


def groups(bits):
    rest = [b for b in range(9) if b not in bits]
    out = []
    for r in range(1 << len(rest)):
        base = sum(((r >> i) & 1) << b for i, b in enumerate(rest))
        members = []
        for k in range(1 << len(bits)):
            members.append(base + sum(((k >> i) & 1) << b for i, b in enumerate(reversed(bits))))
        out.append(members)
    return out


NEAR = groups([8, 5, 4, 3, 0])
FAR = groups([7, 6, 2, 1])


def exchange(pieces, members):
    return lax.all_to_all(pieces, BOTH, 0, 0, tiled=True, axis_index_groups=members)


def swapped(value, axis, phase):
    count = lax.axis_size(axis)
    pairs = []
    for i in range(phase, count - 1, 2):
        pairs += [(i, i + 1), (i + 1, i)]
    return lax.ppermute(value, axis, pairs)


def is_even(axis):
    return lax.rem(lax.axis_index(axis), 2) == 0


def vmem_call(kernel, outs, scratch=(), name=None, anywhere=0):
    space = pl.BlockSpec(memory_space=pltpu.VMEM)

    def call(*args):
        return pl.pallas_call(
            kernel,
            out_shape=tuple(jax.ShapeDtypeStruct(s, t) for s, t in outs),
            in_specs=[space] * (len(args) - anywhere)
            + [pl.BlockSpec(memory_space=pl.ANY)] * anywhere,
            out_specs=tuple(space for _ in outs),
            scratch_shapes=list(scratch),
            compiler_params=pltpu.CompilerParams(vmem_limit_bytes=48 << 20),
            name=name,
        )(*args)

    return call


def edges_kernel(lat, fwd, rev, cots_a, cots_b, row_a, row_b, sems):
    even = is_even("tm")
    head, tail = fwd.at[pl.ds(0, 2)], rev.at[pl.ds(2, 2)]
    at = jnp.where(is_even("tile"), 3, 0)

    @pl.when(even)
    def _():
        pltpu.make_async_copy(tail, cots_a, sems.at[0]).start()
        pltpu.make_async_copy(head, cots_b, sems.at[1]).start()

    @pl.when(jnp.logical_not(even))
    def _():
        pltpu.make_async_copy(head, cots_a, sems.at[0]).start()
        pltpu.make_async_copy(tail, cots_b, sems.at[1]).start()

    pltpu.make_async_copy(lat.at[:, at], row_a, sems.at[2]).start()
    pltpu.make_async_copy(lat.at[:, 3 - at], row_b, sems.at[3]).start()
    pltpu.make_async_copy(head, cots_a, sems.at[0]).wait()
    pltpu.make_async_copy(tail, cots_b, sems.at[1]).wait()
    pltpu.make_async_copy(lat.at[:, at], row_a, sems.at[2]).wait()
    pltpu.make_async_copy(lat.at[:, 3 - at], row_b, sems.at[3]).wait()


def edges(lat, fwd, rev):
    frames, rows, width, channels = lat.shape
    line = (frames, width, channels)
    pair = (2, rows, width, channels)
    return vmem_call(
        edges_kernel,
        [(pair, BF16), (pair, BF16), (line, BF16), (line, BF16)],
        [pltpu.SemaphoreType.DMA((4,))],
        "edges",
        anywhere=3,
    )(lat, fwd, rev)


def spread_columns(row, out, frame, at):
    width = row.shape[0]
    wide = row.astype(F32)
    place = lax.broadcasted_iota(jnp.int32, wide.shape, 0)
    left = jnp.where(place == 0, 0.0, pltpu.roll(wide, 1, 0))
    right = jnp.where(place == width - 1, 0.0, pltpu.roll(wide, width - 1, 0))
    out[frame, at, :, 0:128] = left.astype(BF16)
    out[frame, at, :, 128:256] = row
    out[frame, at, :, 256:384] = right.astype(BF16)


def spread_frame(own, got_a, got_b, even, out, frame):
    one, two = got_a[frame], got_b[frame]
    spread_columns(jnp.where(even, two, one), out, frame, 0)
    for r in range(4):
        spread_columns(own[frame, r], out, frame, r + 1)
    spread_columns(jnp.where(even, one, two), out, frame, 5)


def patch_rows(spread, frame):
    return jnp.concatenate(
        [spread[frame, i : i + 4].reshape(640, 384) for i in range(3)], axis=1
    )


def transposed(block):
    return jnp.transpose(block.astype(F32))


def front_kernel(
    lat, row_a, row_b, fwd, rev, cots_a, cots_b, w_space_at, w_time_at,
    act_out, act_a, act_b, gp, gp_a, gp_b, partial,
    spread, w_space, w_time, back, acc_space, acc_time, sems,
):
    loads = [
        pltpu.make_async_copy(w_time_at, w_time, sems.at[0]),
        pltpu.make_async_copy(w_space_at, w_space, sems.at[1]),
    ]
    for c in loads:
        c.start()
    even_tm, even_tile = is_even("tm"), is_even("tile")
    spread_frame(lat, row_a, row_b, even_tile, spread, 0)
    for c in loads:
        c.wait()
    for k in range(3):
        turned = transposed(w_time[k * 128 : (k + 1) * 128, :]).astype(BF16)
        back[k * 128 : (k + 1) * 128, :] = turned
        back[384 + k * 128 : 384 + (k + 1) * 128, :] = turned
    for f in range(4):
        if f > 0:
            spread_frame(lat, row_a, row_b, even_tile, spread, f)
        patches = patch_rows(spread, f)
        pre = jnp.dot(patches, w_space[...], preferred_element_type=F32)
        sig = 0.5 + 0.5 * jnp.tanh(0.5 * pre)
        act32 = pre * sig
        act = act32.astype(BF16)
        act_out[f] = act.reshape(4, 160, 128)
        cots = []
        for k in range(3):
            if f + k < 4:
                cots.append(fwd[f + k])
            else:
                cots.append(jnp.where(even_tm, cots_a[f + k - 4], cots_b[f + k - 4]))
        for k in range(3):
            if f >= k:
                cots.append(rev[f - k])
            else:
                cots.append(jnp.where(even_tm, cots_b[f - k + 2], cots_a[f - k + 2]))
        cots = jnp.concatenate([c.reshape(640, 128) for c in cots], axis=1)
        grad_act = jnp.dot(cots, back[...], preferred_element_type=F32)
        grad = (grad_act * (sig + act32 * (1.0 - sig))).astype(BF16)
        gp[f] = grad.reshape(4, 160, 128)
        gp_a[f] = jnp.where(even_tile, grad[480:640], grad[0:160])
        gp_b[f] = jnp.where(even_tile, grad[0:160], grad[480:640])
        turn = transposed(grad).astype(BF16)
        more = jnp.dot(turn, patches, preferred_element_type=F32)
        turn = transposed(act).astype(BF16)
        more_time = jnp.dot(turn, cots, preferred_element_type=F32)
        more_time = more_time[:, :384] + more_time[:, 384:]
        if f == 0:
            acc_space[...] = more
            acc_time[...] = more_time
        else:
            acc_space[...] += more
            acc_time[...] += more_time
    for f in range(2):
        act_a[f] = jnp.where(even_tm, act_out[f + 2], act_out[f])
        act_b[f] = jnp.where(even_tm, act_out[f], act_out[f + 2])
    for k in range(9):
        partial[k * 128 : (k + 1) * 128, :] = jnp.transpose(
            acc_space[:, k * 128 : (k + 1) * 128]
        ).astype(BF16)
    for k in range(3):
        partial[(9 + k) * 128 : (10 + k) * 128, :] = acc_time[
            :, k * 128 : (k + 1) * 128
        ].astype(BF16)


def sum_kernel(scale, pieces, out):
    total = pieces[0].astype(F32)
    for k in range(1, pieces.shape[0]):
        total += pieces[k].astype(F32)
    total = (total * scale).astype(BF16)
    for k in range(out.shape[0]):
        out[k] = total


def sum_to_all(pieces, count, scale=1.0):
    (copies,) = vmem_call(
        functools.partial(sum_kernel, scale), [((count, *pieces.shape[1:]), BF16)], (), "share"
    )(pieces)
    return copies


def widen_kernel(pieces, space, time):
    rows = pieces.shape[1]
    for k in range(pieces.shape[0]):
        at = k * rows
        if at < space.shape[0]:
            space[at : at + rows, :] = pieces[k].astype(F32)
        else:
            at -= space.shape[0]
            time[at : at + rows, :] = pieces[k].astype(F32)


def outs_kernel(lat, act, got_a, got_b, w_time, out_f, out_r):
    even = is_even("tm")

    def frame(t):
        if t < 0:
            return jnp.where(even, got_b[t + 2], got_a[t + 2])
        if t < 4:
            return act[t]
        return jnp.where(even, got_a[t - 4], got_b[t - 4])

    for t in range(4):
        residual = lat[t].reshape(640, 128).astype(F32)
        for sign, out in ((-1, out_f), (1, out_r)):
            rows = jnp.concatenate([frame(t + sign * k).reshape(640, 128) for k in range(3)], axis=1)
            total = residual + jnp.dot(rows, w_time[...], preferred_element_type=F32)
            out[t] = total.astype(BF16).reshape(4, 160, 128)


def input_kernel(gp, got_a, got_b, fwd, rev, w_space, out, spread, back):
    even = is_even("tile")
    for i in range(3):
        for j in range(3):
            at = (i * 3 + j) * 128
            back[at : at + 128, :] = transposed(
                w_space[((2 - i) * 3 + 2 - j) * 128 : ((2 - i) * 3 + 3 - j) * 128, :]
            ).astype(BF16)
    for f in range(4):
        spread_frame(gp, got_a, got_b, even, spread, f)
        patches = patch_rows(spread, f)
        total = fwd[f].astype(F32) + rev[f].astype(F32)
        total = total.reshape(640, 128) + jnp.dot(patches, back[...], preferred_element_type=F32)
        out[f] = total.astype(BF16).reshape(4, 160, 128)


def body(latent, cot_forward, cot_reverse, spatial_weight, temporal_weight):
    frame_count, height, width_cells, channels = latent.shape
    cells = latent.shape
    line = (frame_count, width_cells, channels)
    pair = (2, height, width_cells, channels)
    w_space = spatial_weight.reshape(9 * channels, channels)
    w_time = temporal_weight.reshape(3 * channels, channels)
    spread = pltpu.VMEM((frame_count, height + 2, width_cells, 3 * channels), BF16)

    cots_a, cots_b, row_a, row_b = edges(latent, cot_forward, cot_reverse)
    cots_b = swapped(cots_b, "tm", 1)
    cots_a = swapped(cots_a, "tm", 0)
    row_b = swapped(row_b, "tile", 1)
    row_a = swapped(row_a, "tile", 0)
    act, act_a, act_b, gp, gp_a, gp_b, partial = vmem_call(
        front_kernel,
        [
            (cells, BF16), (pair, BF16), (pair, BF16),
            (cells, BF16), (line, BF16), (line, BF16),
            ((12 * channels, channels), BF16),
        ],
        [
            spread,
            pltpu.VMEM((9 * channels, channels), BF16),
            pltpu.VMEM((3 * channels, channels), BF16),
            pltpu.VMEM((6 * channels, channels), BF16),
            pltpu.VMEM((channels, 9 * channels), F32),
            pltpu.VMEM((channels, 3 * channels), F32),
            pltpu.SemaphoreType.DMA((2,)),
        ],
        "front",
        anywhere=2,
    )(latent, row_a, row_b, cot_forward, cot_reverse, cots_a, cots_b, w_space, w_time)

    near, far = len(NEAR[0]), len(FAR[0])
    positions = frame_count * height * width_cells * lax.axis_size("tm") * lax.axis_size("tile")
    shares = sum_to_all(exchange(partial.reshape(near, -1, channels), NEAR), far)
    shares, act_a, act_b, gp_a, gp_b = lax.optimization_barrier((shares, act_a, act_b, gp_a, gp_b))
    shares = exchange(shares, FAR)
    act_b = swapped(act_b, "tm", 1)
    act_a = swapped(act_a, "tm", 0)
    gp_b = swapped(gp_b, "tile", 1)
    gp_a = swapped(gp_a, "tile", 0)
    out_forward, out_reverse = vmem_call(outs_kernel, [(cells, BF16), (cells, BF16)], (), "outs")(
        latent, act, act_a, act_b, w_time
    )
    shares, out_forward, out_reverse, gp_a, gp_b = lax.optimization_barrier(
        (shares, out_forward, out_reverse, gp_a, gp_b)
    )
    whole = exchange(sum_to_all(shares, near, 1.0 / math.sqrt(positions)), NEAR)
    (grad_input,) = vmem_call(
        input_kernel, [(cells, BF16)], [spread, pltpu.VMEM((9 * channels, channels), BF16)], "grad_input"
    )(gp, gp_a, gp_b, cot_forward, cot_reverse, w_space)
    grad_spatial, grad_temporal = vmem_call(
        widen_kernel, [((9 * channels, channels), F32), ((3 * channels, channels), F32)], (), "widen"
    )(whole)
    grad_spatial = grad_spatial.reshape(3, 3, channels, channels)
    grad_temporal = grad_temporal.reshape(3, channels, channels)
    return (out_forward, out_reverse, grad_input, grad_spatial, grad_temporal)


def solution(mesh):
    cells = P("tm", "tile", None, None)
    return jax.shard_map(
        body,
        mesh=mesh,
        in_specs=(cells, cells, cells, P(), P()),
        out_specs=(cells, cells, cells, P(), P()),
        check_vma=False,
    )
```

```python
import functools
import math

import jax
import jax.numpy as jnp
from jax import lax
from jax.experimental import pallas as pl
from jax.experimental.pallas import tpu as pltpu
from jax.sharding import PartitionSpec as P

BOTH = ("tm", "tile")
F32 = jnp.float32
BF16 = jnp.bfloat16


def groups(bits):
    rest = [b for b in range(9) if b not in bits]
    out = []
    for r in range(1 << len(rest)):
        base = sum(((r >> i) & 1) << b for i, b in enumerate(rest))
        members = []
        for k in range(1 << len(bits)):
            members.append(base + sum(((k >> i) & 1) << b for i, b in enumerate(reversed(bits))))
        out.append(members)
    return out


NEAR = groups([8, 5, 4, 3, 0])
FAR = groups([7, 6, 2, 1])


def exchange(pieces, members):
    return lax.all_to_all(pieces, BOTH, 0, 0, tiled=True, axis_index_groups=members)


def swapped(value, axis, phase):
    count = lax.axis_size(axis)
    pairs = []
    for i in range(phase, count - 1, 2):
        pairs += [(i, i + 1), (i + 1, i)]
    return lax.ppermute(value, axis, pairs)


def is_even(axis):
    return lax.rem(lax.axis_index(axis), 2) == 0


def vmem_call(kernel, outs, scratch=(), name=None, in_hbm=0, outs_hbm=()):
    space = pl.BlockSpec(memory_space=pltpu.VMEM)

    def call(*args):
        return pl.pallas_call(
            kernel,
            out_shape=tuple(jax.ShapeDtypeStruct(s, t) for s, t in outs)
            + tuple(pltpu.HBM(s, t) for s, t in outs_hbm),
            in_specs=[space] * (len(args) - in_hbm)
            + [pl.BlockSpec(memory_space=pltpu.HBM)] * in_hbm,
            out_specs=tuple(space for _ in outs)
            + tuple(pl.BlockSpec(memory_space=pltpu.HBM) for _ in outs_hbm),
            scratch_shapes=list(scratch),
            compiler_params=pltpu.CompilerParams(vmem_limit_bytes=48 << 20),
            name=name,
        )(*args[: len(args) - in_hbm], *(held(a) for a in args[len(args) - in_hbm :]))

    return call


def held(value):
    return pltpu.with_memory_space_constraint(value, pltpu.HBM)


def edges_kernel(lat, fwd, rev, cots_a, cots_b, row_a, row_b, sems):
    even = is_even("tm")
    head, tail = fwd.at[pl.ds(0, 2)], rev.at[pl.ds(2, 2)]
    at = jnp.where(is_even("tile"), 3, 0)

    @pl.when(even)
    def _():
        pltpu.make_async_copy(tail, cots_a, sems.at[0]).start()
        pltpu.make_async_copy(head, cots_b, sems.at[1]).start()

    @pl.when(jnp.logical_not(even))
    def _():
        pltpu.make_async_copy(head, cots_a, sems.at[0]).start()
        pltpu.make_async_copy(tail, cots_b, sems.at[1]).start()

    pltpu.make_async_copy(lat.at[:, at], row_a, sems.at[2]).start()
    pltpu.make_async_copy(lat.at[:, 3 - at], row_b, sems.at[3]).start()
    pltpu.make_async_copy(head, cots_a, sems.at[0]).wait()
    pltpu.make_async_copy(tail, cots_b, sems.at[1]).wait()
    pltpu.make_async_copy(lat.at[:, at], row_a, sems.at[2]).wait()
    pltpu.make_async_copy(lat.at[:, 3 - at], row_b, sems.at[3]).wait()


def edges(lat, fwd, rev):
    frames, rows, width, channels = lat.shape
    line = (frames, width, channels)
    pair = (2, rows, width, channels)
    anywhere = pl.BlockSpec(memory_space=pl.ANY)
    return pl.pallas_call(
        edges_kernel,
        out_shape=tuple(jax.ShapeDtypeStruct(s, BF16) for s in (pair, pair, line, line)),
        in_specs=[anywhere] * 3,
        out_specs=(pl.BlockSpec(memory_space=pltpu.VMEM),) * 4,
        scratch_shapes=[pltpu.SemaphoreType.DMA((4,))],
        name="edges",
    )(held(lat), held(fwd), held(rev))


def spread_columns(row, out, frame, at):
    width = row.shape[0]
    wide = row.astype(F32)
    place = lax.broadcasted_iota(jnp.int32, wide.shape, 0)
    left = jnp.where(place == 0, 0.0, pltpu.roll(wide, 1, 0))
    right = jnp.where(place == width - 1, 0.0, pltpu.roll(wide, width - 1, 0))
    out[frame, at, :, 0:128] = left.astype(BF16)
    out[frame, at, :, 128:256] = row
    out[frame, at, :, 256:384] = right.astype(BF16)


def spread_frame(own, got_a, got_b, even, out, frame):
    one, two = got_a[frame], got_b[frame]
    spread_columns(jnp.where(even, two, one), out, frame, 0)
    for r in range(4):
        spread_columns(own[frame, r], out, frame, r + 1)
    spread_columns(jnp.where(even, one, two), out, frame, 5)


def patch_rows(spread, frame):
    return jnp.concatenate(
        [spread[frame, i : i + 4].reshape(640, 384) for i in range(3)], axis=1
    )


def transposed(block):
    return jnp.transpose(block.astype(F32))


def front_kernel(
    lat, row_b, row_a, fwd, rev, cots_b, cots_a, w_space_at, w_time_at,
    act_out, gp_out, act_a, act_b, gp_a, gp_b, partial,
    spread, gp, w_space, w_time, back, acc_space, acc_time, summed, sems,
):
    loads = [
        pltpu.make_async_copy(w_time_at, w_time, sems.at[0]),
        pltpu.make_async_copy(w_space_at, w_space, sems.at[1]),
    ]
    for c in loads:
        c.start()
    even_tm, even_tile = is_even("tm"), is_even("tile")
    spread_frame(lat, row_a, row_b, even_tile, spread, 0)
    for c in loads:
        c.wait()
    for k in range(3):
        turned = transposed(w_time[k * 128 : (k + 1) * 128, :]).astype(BF16)
        back[k * 128 : (k + 1) * 128, :] = turned
        back[384 + k * 128 : 384 + (k + 1) * 128, :] = turned
    stores = []
    for f in range(4):
        if f > 0:
            spread_frame(lat, row_a, row_b, even_tile, spread, f)
        patches = patch_rows(spread, f)
        pre = jnp.dot(patches, w_space[...], preferred_element_type=F32)
        sig = 0.5 + 0.5 * jnp.tanh(0.5 * pre)
        act32 = pre * sig
        act = act32.astype(BF16)
        act_out[f] = act.reshape(4, 160, 128)
        cots = []
        for k in range(3):
            if f + k < 4:
                cots.append(fwd[f + k])
            else:
                cots.append(jnp.where(even_tm, cots_a[f + k - 4], cots_b[f + k - 4]))
        for k in range(3):
            if f >= k:
                cots.append(rev[f - k])
            else:
                cots.append(jnp.where(even_tm, cots_b[f - k + 2], cots_a[f - k + 2]))
        cots = jnp.concatenate([c.reshape(640, 128) for c in cots], axis=1)
        grad_act = jnp.dot(cots, back[...], preferred_element_type=F32)
        grad = (grad_act * (sig + act32 * (1.0 - sig))).astype(BF16)
        gp[f] = grad.reshape(4, 160, 128)
        gp_copy = pltpu.make_async_copy(gp.at[f], gp_out.at[f], sems.at[7 + f])
        gp_copy.start()
        stores.append(gp_copy)
        turn = transposed(grad).astype(BF16)
        more = jnp.dot(turn, patches, preferred_element_type=F32)
        turn = transposed(act).astype(BF16)
        more_time = jnp.dot(turn, cots, preferred_element_type=F32)
        more_time = more_time[:, :384] + more_time[:, 384:]
        if f == 0:
            acc_space[...] = more
            acc_time[...] = more_time
        else:
            acc_space[...] += more
            acc_time[...] += more_time
    at_frame, at_row = jnp.where(even_tm, 2, 0), jnp.where(even_tile, 3, 0)
    edge_stores = [
        pltpu.make_async_copy(act_out.at[pl.ds(at_frame, 2)], act_a, sems.at[2]),
        pltpu.make_async_copy(act_out.at[pl.ds(2 - at_frame, 2)], act_b, sems.at[3]),
        pltpu.make_async_copy(gp.at[:, at_row], gp_a, sems.at[4]),
        pltpu.make_async_copy(gp.at[:, 3 - at_row], gp_b, sems.at[5]),
    ]
    for c in edge_stores:
        c.start()
    stores += edge_stores
    for k in range(9):
        summed[k * 128 : (k + 1) * 128, :] = jnp.transpose(
            acc_space[:, k * 128 : (k + 1) * 128]
        ).astype(BF16)
    for k in range(3):
        summed[(9 + k) * 128 : (10 + k) * 128, :] = acc_time[
            :, k * 128 : (k + 1) * 128
        ].astype(BF16)
    stores.append(pltpu.make_async_copy(summed, partial, sems.at[6]))
    stores[-1].start()
    for c in stores:
        c.wait()


def sum_kernel(scale, pieces, out):
    total = pieces[0].astype(F32)
    for k in range(1, pieces.shape[0]):
        total += pieces[k].astype(F32)
    total = (total * scale).astype(BF16)
    for k in range(out.shape[0]):
        out[k] = total


def sum_to_all(pieces, count, scale=1.0):
    (copies,) = vmem_call(
        functools.partial(sum_kernel, scale), [((count, *pieces.shape[1:]), BF16)], (), "share"
    )(pieces)
    return copies


def widen_kernel(pieces, space, time):
    rows = pieces.shape[1]
    for k in range(pieces.shape[0]):
        at = k * rows
        if at < space.shape[0]:
            space[at : at + rows, :] = pieces[k].astype(F32)
        else:
            at -= space.shape[0]
            time[at : at + rows, :] = pieces[k].astype(F32)


def outs_kernel(lat, act, got_b, got_a, w_time, out_f, out_r):
    even = is_even("tm")

    def frame(t):
        if t < 0:
            return jnp.where(even, got_b[t + 2], got_a[t + 2])
        if t < 4:
            return act[t]
        return jnp.where(even, got_a[t - 4], got_b[t - 4])

    for t in range(4):
        residual = lat[t].reshape(640, 128).astype(F32)
        for sign, out in ((-1, out_f), (1, out_r)):
            rows = jnp.concatenate([frame(t + sign * k).reshape(640, 128) for k in range(3)], axis=1)
            total = residual + jnp.dot(rows, w_time[...], preferred_element_type=F32)
            out[t] = total.astype(BF16).reshape(4, 160, 128)


def input_kernel(gp, got_b, got_a, fwd, rev, w_space, out, spread, back):
    even = is_even("tile")
    for i in range(3):
        for j in range(3):
            at = (i * 3 + j) * 128
            back[at : at + 128, :] = transposed(
                w_space[((2 - i) * 3 + 2 - j) * 128 : ((2 - i) * 3 + 3 - j) * 128, :]
            ).astype(BF16)
    for f in range(4):
        spread_frame(gp, got_a, got_b, even, spread, f)
        patches = patch_rows(spread, f)
        total = fwd[f].astype(F32) + rev[f].astype(F32)
        total = total.reshape(640, 128) + jnp.dot(patches, back[...], preferred_element_type=F32)
        out[f] = total.astype(BF16).reshape(4, 160, 128)


def body(latent, cot_forward, cot_reverse, spatial_weight, temporal_weight):
    frame_count, height, width_cells, channels = latent.shape
    cells = latent.shape
    line = (frame_count, width_cells, channels)
    pair = (2, height, width_cells, channels)
    w_space = spatial_weight.reshape(9 * channels, channels)
    w_time = temporal_weight.reshape(3 * channels, channels)
    spread = pltpu.VMEM((frame_count, height + 2, width_cells, 3 * channels), BF16)

    cots_a, cots_b, row_a, row_b = edges(latent, cot_forward, cot_reverse)
    cots_b = swapped(cots_b, "tm", 1)
    cots_a = swapped(cots_a, "tm", 0)
    row_b = swapped(row_b, "tile", 1)
    row_a = swapped(row_a, "tile", 0)
    act, gp, act_a, act_b, gp_a, gp_b, partial = vmem_call(
        front_kernel,
        [(cells, BF16)],
        [
            spread,
            pltpu.VMEM(cells, BF16),
            pltpu.VMEM((9 * channels, channels), BF16),
            pltpu.VMEM((3 * channels, channels), BF16),
            pltpu.VMEM((6 * channels, channels), BF16),
            pltpu.VMEM((channels, 9 * channels), F32),
            pltpu.VMEM((channels, 3 * channels), F32),
            pltpu.VMEM((12 * channels, channels), BF16),
            pltpu.SemaphoreType.DMA((11,)),
        ],
        "front",
        in_hbm=2,
        outs_hbm=[(cells, BF16)] + [(pair, BF16)] * 2 + [(line, BF16)] * 2 + [((12 * channels, channels), BF16)],
    )(latent, row_b, row_a, cot_forward, cot_reverse, cots_b, cots_a, w_space, w_time)

    near, far = len(NEAR[0]), len(FAR[0])
    positions = frame_count * height * width_cells * lax.axis_size("tm") * lax.axis_size("tile")
    shares = sum_to_all(exchange(partial.reshape(near, -1, channels), NEAR), far)
    act_b = swapped(act_b, "tm", 1)
    act_a = swapped(act_a, "tm", 0)
    shares, gp_b, gp_a, act_b, act_a = lax.optimization_barrier((shares, gp_b, gp_a, act_b, act_a))
    shares = exchange(shares, FAR)
    gp_b = swapped(gp_b, "tile", 1)
    gp_a = swapped(gp_a, "tile", 0)
    out_forward, out_reverse = vmem_call(outs_kernel, [(cells, BF16), (cells, BF16)], (), "outs")(
        latent, act, act_b, act_a, w_time
    )
    shares, out_forward, out_reverse, gp_b, gp_a = lax.optimization_barrier(
        (shares, out_forward, out_reverse, gp_b, gp_a)
    )
    whole = exchange(sum_to_all(shares, near, 1.0 / math.sqrt(positions)), NEAR)
    (grad_input,) = vmem_call(
        input_kernel, [(cells, BF16)], [spread, pltpu.VMEM((9 * channels, channels), BF16)], "grad_input"
    )(gp, gp_b, gp_a, cot_forward, cot_reverse, w_space)
    grad_spatial, grad_temporal = vmem_call(
        widen_kernel, [((9 * channels, channels), F32), ((3 * channels, channels), F32)], (), "widen"
    )(whole)
    grad_spatial = grad_spatial.reshape(3, 3, channels, channels)
    grad_temporal = grad_temporal.reshape(3, channels, channels)
    return (out_forward, out_reverse, grad_input, grad_spatial, grad_temporal)


def solution(mesh):
    cells = P("tm", "tile", None, None)
    return jax.shard_map(
        body,
        mesh=mesh,
        in_specs=(cells, cells, cells, P(), P()),
        out_specs=(cells, cells, cells, P(), P()),
        check_vma=False,
    )
```

```python
import functools
import math

import jax
import jax.numpy as jnp
from jax import lax
from jax.experimental import pallas as pl
from jax.experimental.pallas import tpu as pltpu
from jax.sharding import PartitionSpec as P

BOTH = ("tm", "tile")
F32 = jnp.float32
BF16 = jnp.bfloat16


def groups(bits):
    rest = [b for b in range(9) if b not in bits]
    out = []
    for r in range(1 << len(rest)):
        base = sum(((r >> i) & 1) << b for i, b in enumerate(rest))
        members = []
        for k in range(1 << len(bits)):
            members.append(base + sum(((k >> i) & 1) << b for i, b in enumerate(reversed(bits))))
        out.append(members)
    return out


NEAR = groups([8, 5, 4, 3, 0])
FAR = groups([7, 6, 2, 1])


def exchange(pieces, members):
    return lax.all_to_all(pieces, BOTH, 0, 0, tiled=True, axis_index_groups=members)


def swapped(value, axis, phase):
    count = lax.axis_size(axis)
    pairs = []
    for i in range(phase, count - 1, 2):
        pairs += [(i, i + 1), (i + 1, i)]
    return lax.ppermute(value, axis, pairs)


def is_even(axis):
    return lax.rem(lax.axis_index(axis), 2) == 0


def vmem_call(kernel, outs, scratch=(), name=None, in_hbm=0, outs_hbm=()):
    space = pl.BlockSpec(memory_space=pltpu.VMEM)

    def call(*args):
        return pl.pallas_call(
            kernel,
            out_shape=tuple(jax.ShapeDtypeStruct(s, t) for s, t in outs)
            + tuple(pltpu.HBM(s, t) for s, t in outs_hbm),
            in_specs=[space] * (len(args) - in_hbm)
            + [pl.BlockSpec(memory_space=pltpu.HBM)] * in_hbm,
            out_specs=tuple(space for _ in outs)
            + tuple(pl.BlockSpec(memory_space=pltpu.HBM) for _ in outs_hbm),
            scratch_shapes=list(scratch),
            compiler_params=pltpu.CompilerParams(vmem_limit_bytes=48 << 20),
            name=name,
        )(*args[: len(args) - in_hbm], *(held(a) for a in args[len(args) - in_hbm :]))

    return call


def held(value):
    return pltpu.with_memory_space_constraint(value, pltpu.HBM)


def edges_kernel(lat, fwd, rev, cots_a, cots_b, row_a, row_b, sems):
    even = is_even("tm")
    head, tail = fwd.at[pl.ds(0, 2)], rev.at[pl.ds(2, 2)]
    at = jnp.where(is_even("tile"), 3, 0)

    @pl.when(even)
    def _():
        pltpu.make_async_copy(tail, cots_a, sems.at[0]).start()
        pltpu.make_async_copy(head, cots_b, sems.at[1]).start()

    @pl.when(jnp.logical_not(even))
    def _():
        pltpu.make_async_copy(head, cots_a, sems.at[0]).start()
        pltpu.make_async_copy(tail, cots_b, sems.at[1]).start()

    pltpu.make_async_copy(lat.at[:, at], row_a, sems.at[2]).start()
    pltpu.make_async_copy(lat.at[:, 3 - at], row_b, sems.at[3]).start()
    pltpu.make_async_copy(head, cots_a, sems.at[0]).wait()
    pltpu.make_async_copy(tail, cots_b, sems.at[1]).wait()
    pltpu.make_async_copy(lat.at[:, at], row_a, sems.at[2]).wait()
    pltpu.make_async_copy(lat.at[:, 3 - at], row_b, sems.at[3]).wait()


def edges(lat, fwd, rev):
    frames, rows, width, channels = lat.shape
    line = (frames, width, channels)
    pair = (2, rows, width, channels)
    anywhere = pl.BlockSpec(memory_space=pl.ANY)
    return pl.pallas_call(
        edges_kernel,
        out_shape=tuple(jax.ShapeDtypeStruct(s, BF16) for s in (pair, pair, line, line)),
        in_specs=[anywhere] * 3,
        out_specs=(pl.BlockSpec(memory_space=pltpu.VMEM),) * 4,
        scratch_shapes=[pltpu.SemaphoreType.DMA((4,))],
        name="edges",
    )(held(lat), held(fwd), held(rev))


def spread_columns(row, out, frame, at):
    width = row.shape[0]
    wide = row.astype(F32)
    place = lax.broadcasted_iota(jnp.int32, wide.shape, 0)
    left = jnp.where(place == 0, 0.0, pltpu.roll(wide, 1, 0))
    right = jnp.where(place == width - 1, 0.0, pltpu.roll(wide, width - 1, 0))
    out[frame, at, :, 0:128] = left.astype(BF16)
    out[frame, at, :, 128:256] = row
    out[frame, at, :, 256:384] = right.astype(BF16)


def spread_frame(own, got_a, got_b, even, out, frame):
    one, two = got_a[frame], got_b[frame]
    spread_columns(jnp.where(even, two, one), out, frame, 0)
    for r in range(4):
        spread_columns(own[frame, r], out, frame, r + 1)
    spread_columns(jnp.where(even, one, two), out, frame, 5)


def patch_rows(spread, frame):
    return jnp.concatenate(
        [spread[frame, i : i + 4].reshape(640, 384) for i in range(3)], axis=1
    )


def transposed(block):
    return jnp.transpose(block.astype(F32))


def front_kernel(
    lat, row_b, row_a, fwd, rev, cots_b, cots_a, w_space_at, w_time_at,
    act_out, gp_out, act_a, act_b, gp_a, gp_b, partial,
    spread, gp, w_space, w_time, back, acc_space, acc_time, summed, sems,
):
    loads = [
        pltpu.make_async_copy(w_time_at, w_time, sems.at[0]),
        pltpu.make_async_copy(w_space_at, w_space, sems.at[1]),
    ]
    for c in loads:
        c.start()
    even_tm, even_tile = is_even("tm"), is_even("tile")
    spread_frame(lat, row_a, row_b, even_tile, spread, 0)
    for c in loads:
        c.wait()
    for k in range(3):
        turned = transposed(w_time[k * 128 : (k + 1) * 128, :]).astype(BF16)
        back[k * 128 : (k + 1) * 128, :] = turned
        back[384 + k * 128 : 384 + (k + 1) * 128, :] = turned
    stores = []
    for f in range(4):
        if f > 0:
            spread_frame(lat, row_a, row_b, even_tile, spread, f)
        patches = patch_rows(spread, f)
        pre = jnp.dot(patches, w_space[...], preferred_element_type=F32)
        sig = 0.5 + 0.5 * jnp.tanh(0.5 * pre)
        act32 = pre * sig
        act = act32.astype(BF16)
        act_out[f] = act.reshape(4, 160, 128)
        cots = []
        for k in range(3):
            if f + k < 4:
                cots.append(fwd[f + k])
            else:
                cots.append(jnp.where(even_tm, cots_a[f + k - 4], cots_b[f + k - 4]))
        for k in range(3):
            if f >= k:
                cots.append(rev[f - k])
            else:
                cots.append(jnp.where(even_tm, cots_b[f - k + 2], cots_a[f - k + 2]))
        cots = jnp.concatenate([c.reshape(640, 128) for c in cots], axis=1)
        grad_act = jnp.dot(cots, back[...], preferred_element_type=F32)
        grad = (grad_act * (sig + act32 * (1.0 - sig))).astype(BF16)
        gp[f] = grad.reshape(4, 160, 128)
        gp_copy = pltpu.make_async_copy(gp.at[f], gp_out.at[f], sems.at[7 + f])
        gp_copy.start()
        stores.append(gp_copy)
        turn = transposed(grad).astype(BF16)
        more = jnp.dot(turn, patches, preferred_element_type=F32)
        turn = transposed(act).astype(BF16)
        more_time = jnp.dot(turn, cots, preferred_element_type=F32)
        more_time = more_time[:, :384] + more_time[:, 384:]
        if f == 0:
            acc_space[...] = more
            acc_time[...] = more_time
        else:
            acc_space[...] += more
            acc_time[...] += more_time
    at_frame, at_row = jnp.where(even_tm, 2, 0), jnp.where(even_tile, 3, 0)
    edge_stores = [
        pltpu.make_async_copy(act_out.at[pl.ds(at_frame, 2)], act_a, sems.at[2]),
        pltpu.make_async_copy(act_out.at[pl.ds(2 - at_frame, 2)], act_b, sems.at[3]),
        pltpu.make_async_copy(gp.at[:, at_row], gp_a, sems.at[4]),
        pltpu.make_async_copy(gp.at[:, 3 - at_row], gp_b, sems.at[5]),
    ]
    for c in edge_stores:
        c.start()
    stores += edge_stores
    for k in range(3):
        summed[(9 + k) * 128 : (10 + k) * 128, :] = acc_time[:, k * 128 : (k + 1) * 128].astype(BF16)
    for part in (3, 0, 1, 2):
        if part < 3:
            for k in range(part * 3, part * 3 + 3):
                summed[k * 128 : (k + 1) * 128, :] = jnp.transpose(
                    acc_space[:, k * 128 : (k + 1) * 128]
                ).astype(BF16)
        rows = pl.ds(part * 384, 384)
        stores.append(pltpu.make_async_copy(summed.at[rows], partial.at[rows], sems.at[11 + part]))
        stores[-1].start()
    for c in stores:
        c.wait()


def sum_kernel(scale, pieces, out):
    total = pieces[0].astype(F32)
    for k in range(1, pieces.shape[0]):
        total += pieces[k].astype(F32)
    total = (total * scale).astype(BF16)
    for k in range(out.shape[0]):
        out[k] = total


def sum_to_all(pieces, count, scale=1.0):
    (copies,) = vmem_call(
        functools.partial(sum_kernel, scale), [((count, *pieces.shape[1:]), BF16)], (), "share"
    )(pieces)
    return copies


def widen_kernel(pieces, space, time):
    rows = pieces.shape[1]
    for k in range(pieces.shape[0]):
        at = k * rows
        if at < space.shape[0]:
            space[at : at + rows, :] = pieces[k].astype(F32)
        else:
            at -= space.shape[0]
            time[at : at + rows, :] = pieces[k].astype(F32)


def outs_kernel(lat, act, got_b, got_a, w_time, out_f, out_r):
    even = is_even("tm")

    def frame(t):
        if t < 0:
            return jnp.where(even, got_b[t + 2], got_a[t + 2])
        if t < 4:
            return act[t]
        return jnp.where(even, got_a[t - 4], got_b[t - 4])

    for t in range(4):
        residual = lat[t].reshape(640, 128).astype(F32)
        for sign, out in ((-1, out_f), (1, out_r)):
            rows = jnp.concatenate([frame(t + sign * k).reshape(640, 128) for k in range(3)], axis=1)
            total = residual + jnp.dot(rows, w_time[...], preferred_element_type=F32)
            out[t] = total.astype(BF16).reshape(4, 160, 128)


def input_kernel(gp, got_b, got_a, fwd, rev, w_space, out, spread, back):
    even = is_even("tile")
    for i in range(3):
        for j in range(3):
            at = (i * 3 + j) * 128
            back[at : at + 128, :] = transposed(
                w_space[((2 - i) * 3 + 2 - j) * 128 : ((2 - i) * 3 + 3 - j) * 128, :]
            ).astype(BF16)
    for f in range(4):
        spread_frame(gp, got_a, got_b, even, spread, f)
        patches = patch_rows(spread, f)
        total = fwd[f].astype(F32) + rev[f].astype(F32)
        total = total.reshape(640, 128) + jnp.dot(patches, back[...], preferred_element_type=F32)
        out[f] = total.astype(BF16).reshape(4, 160, 128)


def body(latent, cot_forward, cot_reverse, spatial_weight, temporal_weight):
    frame_count, height, width_cells, channels = latent.shape
    cells = latent.shape
    line = (frame_count, width_cells, channels)
    pair = (2, height, width_cells, channels)
    w_space = spatial_weight.reshape(9 * channels, channels)
    w_time = temporal_weight.reshape(3 * channels, channels)
    spread = pltpu.VMEM((frame_count, height + 2, width_cells, 3 * channels), BF16)

    cots_a, cots_b, row_a, row_b = edges(latent, cot_forward, cot_reverse)
    cots_b = swapped(cots_b, "tm", 1)
    cots_a = swapped(cots_a, "tm", 0)
    row_b = swapped(row_b, "tile", 1)
    row_a = swapped(row_a, "tile", 0)
    act, gp, act_a, act_b, gp_a, gp_b, partial = vmem_call(
        front_kernel,
        [(cells, BF16)],
        [
            spread,
            pltpu.VMEM(cells, BF16),
            pltpu.VMEM((9 * channels, channels), BF16),
            pltpu.VMEM((3 * channels, channels), BF16),
            pltpu.VMEM((6 * channels, channels), BF16),
            pltpu.VMEM((channels, 9 * channels), F32),
            pltpu.VMEM((channels, 3 * channels), F32),
            pltpu.VMEM((12 * channels, channels), BF16),
            pltpu.SemaphoreType.DMA((15,)),
        ],
        "front",
        in_hbm=2,
        outs_hbm=[(cells, BF16)] + [(pair, BF16)] * 2 + [(line, BF16)] * 2 + [((12 * channels, channels), BF16)],
    )(latent, row_b, row_a, cot_forward, cot_reverse, cots_b, cots_a, w_space, w_time)

    near, far = len(NEAR[0]), len(FAR[0])
    positions = frame_count * height * width_cells * lax.axis_size("tm") * lax.axis_size("tile")
    shares = sum_to_all(exchange(partial.reshape(near, -1, channels), NEAR), far)
    act_b = swapped(act_b, "tm", 1)
    act_a = swapped(act_a, "tm", 0)
    out_forward, out_reverse = vmem_call(outs_kernel, [(cells, BF16), (cells, BF16)], (), "outs")(
        latent, act, act_b, act_a, w_time
    )
    gp_b, gp_a, out_forward, out_reverse = lax.optimization_barrier((gp_b, gp_a, out_forward, out_reverse))
    gp_b = swapped(gp_b, "tile", 1)
    gp_a = swapped(gp_a, "tile", 0)
    shares = exchange(shares, FAR)
    shares, gp_b, gp_a = lax.optimization_barrier((shares, gp_b, gp_a))
    shares = sum_to_all(shares, near, 1.0 / math.sqrt(positions))
    whole = exchange(shares, NEAR)
    (grad_input,) = vmem_call(
        input_kernel, [(cells, BF16)], [spread, pltpu.VMEM((9 * channels, channels), BF16)], "grad_input"
    )(gp, gp_b, gp_a, cot_forward, cot_reverse, w_space)
    grad_spatial, grad_temporal = vmem_call(
        widen_kernel, [((9 * channels, channels), F32), ((3 * channels, channels), F32)], (), "widen"
    )(whole)
    grad_spatial = grad_spatial.reshape(3, 3, channels, channels)
    grad_temporal = grad_temporal.reshape(3, channels, channels)
    return (out_forward, out_reverse, grad_input, grad_spatial, grad_temporal)


def solution(mesh):
    cells = P("tm", "tile", None, None)
    return jax.shard_map(
        body,
        mesh=mesh,
        in_specs=(cells, cells, cells, P(), P()),
        out_specs=(cells, cells, cells, P(), P()),
        check_vma=False,
    )
```

```python
import functools
import math

import jax
import jax.numpy as jnp
from jax import lax
from jax.experimental import pallas as pl
from jax.experimental.pallas import tpu as pltpu
from jax.sharding import PartitionSpec as P

BOTH = ("tm", "tile")
F32 = jnp.float32
BF16 = jnp.bfloat16


def groups(bits):
    rest = [b for b in range(9) if b not in bits]
    out = []
    for r in range(1 << len(rest)):
        base = sum(((r >> i) & 1) << b for i, b in enumerate(rest))
        members = []
        for k in range(1 << len(bits)):
            members.append(base + sum(((k >> i) & 1) << b for i, b in enumerate(reversed(bits))))
        out.append(members)
    return out


NEAR = groups([8, 5, 4, 3, 0])
FAR = groups([7, 6, 2, 1])


def exchange(pieces, members):
    return lax.all_to_all(pieces, BOTH, 0, 0, tiled=True, axis_index_groups=members)


def swapped(value, axis, phase):
    count = lax.axis_size(axis)
    pairs = []
    for i in range(phase, count - 1, 2):
        pairs += [(i, i + 1), (i + 1, i)]
    return lax.ppermute(value, axis, pairs)


def is_even(axis):
    return lax.rem(lax.axis_index(axis), 2) == 0


def vmem_call(kernel, outs, scratch=(), name=None, in_hbm=0, outs_hbm=(), cost=None):
    space = pl.BlockSpec(memory_space=pltpu.VMEM)

    def call(*args):
        return pl.pallas_call(
            kernel,
            out_shape=tuple(jax.ShapeDtypeStruct(s, t) for s, t in outs)
            + tuple(pltpu.HBM(s, t) for s, t in outs_hbm),
            in_specs=[space] * (len(args) - in_hbm)
            + [pl.BlockSpec(memory_space=pltpu.HBM)] * in_hbm,
            out_specs=tuple(space for _ in outs)
            + tuple(pl.BlockSpec(memory_space=pltpu.HBM) for _ in outs_hbm),
            scratch_shapes=list(scratch),
            compiler_params=pltpu.CompilerParams(vmem_limit_bytes=48 << 20),
            name=name,
            cost_estimate=cost,
        )(*args[: len(args) - in_hbm], *(held(a) for a in args[len(args) - in_hbm :]))

    return call


def held(value):
    return pltpu.with_memory_space_constraint(value, pltpu.HBM)


def edges_kernel(lat, fwd, rev, cots_a, cots_b, row_a, row_b, sems):
    even = is_even("tm")
    head, tail = fwd.at[pl.ds(0, 2)], rev.at[pl.ds(2, 2)]
    at = jnp.where(is_even("tile"), 3, 0)

    @pl.when(even)
    def _():
        pltpu.make_async_copy(tail, cots_a, sems.at[0]).start()
        pltpu.make_async_copy(head, cots_b, sems.at[1]).start()

    @pl.when(jnp.logical_not(even))
    def _():
        pltpu.make_async_copy(head, cots_a, sems.at[0]).start()
        pltpu.make_async_copy(tail, cots_b, sems.at[1]).start()

    pltpu.make_async_copy(lat.at[:, at], row_a, sems.at[2]).start()
    pltpu.make_async_copy(lat.at[:, 3 - at], row_b, sems.at[3]).start()
    pltpu.make_async_copy(head, cots_a, sems.at[0]).wait()
    pltpu.make_async_copy(tail, cots_b, sems.at[1]).wait()
    pltpu.make_async_copy(lat.at[:, at], row_a, sems.at[2]).wait()
    pltpu.make_async_copy(lat.at[:, 3 - at], row_b, sems.at[3]).wait()


def edges(lat, fwd, rev):
    frames, rows, width, channels = lat.shape
    line = (frames, width, channels)
    pair = (2, rows, width, channels)
    anywhere = pl.BlockSpec(memory_space=pl.ANY)
    return pl.pallas_call(
        edges_kernel,
        out_shape=tuple(jax.ShapeDtypeStruct(s, BF16) for s in (pair, pair, line, line)),
        in_specs=[anywhere] * 3,
        out_specs=(pl.BlockSpec(memory_space=pltpu.VMEM),) * 4,
        scratch_shapes=[pltpu.SemaphoreType.DMA((4,))],
        name="edges",
    )(held(lat), held(fwd), held(rev))


def spread_columns(row, out, frame, at):
    width = row.shape[0]
    wide = row.astype(F32)
    place = lax.broadcasted_iota(jnp.int32, wide.shape, 0)
    left = jnp.where(place == 0, 0.0, pltpu.roll(wide, 1, 0))
    right = jnp.where(place == width - 1, 0.0, pltpu.roll(wide, width - 1, 0))
    out[frame, at, :, 0:128] = left.astype(BF16)
    out[frame, at, :, 128:256] = row
    out[frame, at, :, 256:384] = right.astype(BF16)


def spread_frame(own, got_a, got_b, even, out, frame):
    one, two = got_a[frame], got_b[frame]
    spread_columns(jnp.where(even, two, one), out, frame, 0)
    for r in range(4):
        spread_columns(own[frame, r], out, frame, r + 1)
    spread_columns(jnp.where(even, one, two), out, frame, 5)


def patch_rows(spread, frame):
    return jnp.concatenate(
        [spread[frame, i : i + 4].reshape(640, 384) for i in range(3)], axis=1
    )


def transposed(block):
    return jnp.transpose(block.astype(F32))


def front_kernel(
    lat, row_b, row_a, fwd, rev, cots_b, cots_a, w_space_at, w_time_at,
    act_out, gp_out, act_a, act_b, gp_a, gp_b, partial,
    spread, gp, w_space, w_time, back, acc_space, acc_time, summed, sems,
):
    loads = [
        pltpu.make_async_copy(w_time_at, w_time, sems.at[0]),
        pltpu.make_async_copy(w_space_at, w_space, sems.at[1]),
    ]
    for c in loads:
        c.start()
    even_tm, even_tile = is_even("tm"), is_even("tile")
    spread_frame(lat, row_a, row_b, even_tile, spread, 0)
    for c in loads:
        c.wait()
    for k in range(3):
        turned = transposed(w_time[k * 128 : (k + 1) * 128, :]).astype(BF16)
        back[k * 128 : (k + 1) * 128, :] = turned
        back[384 + k * 128 : 384 + (k + 1) * 128, :] = turned
    stores = []
    for f in range(4):
        if f > 0:
            spread_frame(lat, row_a, row_b, even_tile, spread, f)
        patches = patch_rows(spread, f)
        pre = jnp.dot(patches, w_space[...], preferred_element_type=F32)
        sig = 0.5 + 0.5 * jnp.tanh(0.5 * pre)
        act32 = pre * sig
        act = act32.astype(BF16)
        act_out[f] = act.reshape(4, 160, 128)
        cots = []
        for k in range(3):
            if f + k < 4:
                cots.append(fwd[f + k])
            else:
                cots.append(jnp.where(even_tm, cots_a[f + k - 4], cots_b[f + k - 4]))
        for k in range(3):
            if f >= k:
                cots.append(rev[f - k])
            else:
                cots.append(jnp.where(even_tm, cots_b[f - k + 2], cots_a[f - k + 2]))
        cots = jnp.concatenate([c.reshape(640, 128) for c in cots], axis=1)
        grad_act = jnp.dot(cots, back[...], preferred_element_type=F32)
        grad = (grad_act * (sig + act32 * (1.0 - sig))).astype(BF16)
        gp[f] = grad.reshape(4, 160, 128)
        gp_copy = pltpu.make_async_copy(gp.at[f], gp_out.at[f], sems.at[7 + f])
        gp_copy.start()
        stores.append(gp_copy)
        turn = transposed(grad).astype(BF16)
        more = jnp.dot(turn, patches, preferred_element_type=F32)
        turn = transposed(act).astype(BF16)
        more_time = jnp.dot(turn, cots, preferred_element_type=F32)
        more_time = more_time[:, :384] + more_time[:, 384:]
        if f == 0:
            acc_space[...] = more
            acc_time[...] = more_time
        else:
            acc_space[...] += more
            acc_time[...] += more_time
    at_frame, at_row = jnp.where(even_tm, 2, 0), jnp.where(even_tile, 3, 0)
    edge_stores = [
        pltpu.make_async_copy(act_out.at[pl.ds(at_frame, 2)], act_a, sems.at[2]),
        pltpu.make_async_copy(act_out.at[pl.ds(2 - at_frame, 2)], act_b, sems.at[3]),
        pltpu.make_async_copy(gp.at[:, at_row], gp_a, sems.at[4]),
        pltpu.make_async_copy(gp.at[:, 3 - at_row], gp_b, sems.at[5]),
    ]
    for c in edge_stores:
        c.start()
    stores += edge_stores
    for k in range(3):
        summed[(9 + k) * 128 : (10 + k) * 128, :] = acc_time[:, k * 128 : (k + 1) * 128].astype(BF16)
    for part in (3, 0, 1, 2):
        if part < 3:
            for k in range(part * 3, part * 3 + 3):
                summed[k * 128 : (k + 1) * 128, :] = jnp.transpose(
                    acc_space[:, k * 128 : (k + 1) * 128]
                ).astype(BF16)
        rows = pl.ds(part * 384, 384)
        stores.append(pltpu.make_async_copy(summed.at[rows], partial.at[rows], sems.at[11 + part]))
        stores[-1].start()
    for c in stores:
        c.wait()


def sum_kernel(scale, pieces, out):
    total = pieces[0].astype(F32)
    for k in range(1, pieces.shape[0]):
        total += pieces[k].astype(F32)
    total = (total * scale).astype(BF16)
    for k in range(out.shape[0]):
        out[k] = total


def sum_to_all(pieces, count, scale=1.0):
    (copies,) = vmem_call(
        functools.partial(sum_kernel, scale), [((count, *pieces.shape[1:]), BF16)], (), "share"
    )(pieces)
    return copies


def widen_kernel(pieces, space, time):
    rows = pieces.shape[1]
    for k in range(pieces.shape[0]):
        at = k * rows
        if at < space.shape[0]:
            space[at : at + rows, :] = pieces[k].astype(F32)
        else:
            at -= space.shape[0]
            time[at : at + rows, :] = pieces[k].astype(F32)


def outs_kernel(lat, act, got_b, got_a, w_time, out_f, out_r):
    even = is_even("tm")

    def frame(t):
        if t < 0:
            return jnp.where(even, got_b[t + 2], got_a[t + 2])
        if t < 4:
            return act[t]
        return jnp.where(even, got_a[t - 4], got_b[t - 4])

    for t in range(4):
        residual = lat[t].reshape(640, 128).astype(F32)
        for sign, out in ((-1, out_f), (1, out_r)):
            rows = jnp.concatenate([frame(t + sign * k).reshape(640, 128) for k in range(3)], axis=1)
            total = residual + jnp.dot(rows, w_time[...], preferred_element_type=F32)
            out[t] = total.astype(BF16).reshape(4, 160, 128)


def input_kernel(gp, got_b, got_a, fwd, rev, w_space, out, spread, back):
    even = is_even("tile")
    for i in range(3):
        for j in range(3):
            at = (i * 3 + j) * 128
            back[at : at + 128, :] = transposed(
                w_space[((2 - i) * 3 + 2 - j) * 128 : ((2 - i) * 3 + 3 - j) * 128, :]
            ).astype(BF16)
    for f in range(4):
        spread_frame(gp, got_a, got_b, even, spread, f)
        patches = patch_rows(spread, f)
        total = fwd[f].astype(F32) + rev[f].astype(F32)
        total = total.reshape(640, 128) + jnp.dot(patches, back[...], preferred_element_type=F32)
        out[f] = total.astype(BF16).reshape(4, 160, 128)


def body(latent, cot_forward, cot_reverse, spatial_weight, temporal_weight):
    frame_count, height, width_cells, channels = latent.shape
    cells = latent.shape
    line = (frame_count, width_cells, channels)
    pair = (2, height, width_cells, channels)
    w_space = spatial_weight.reshape(9 * channels, channels)
    w_time = temporal_weight.reshape(3 * channels, channels)
    spread = pltpu.VMEM((frame_count, height + 2, width_cells, 3 * channels), BF16)

    cots_a, cots_b, row_a, row_b = edges(latent, cot_forward, cot_reverse)
    cots_b = swapped(cots_b, "tm", 1)
    cots_a = swapped(cots_a, "tm", 0)
    row_b = swapped(row_b, "tile", 1)
    row_a = swapped(row_a, "tile", 0)
    act, gp, act_a, act_b, gp_a, gp_b, partial = vmem_call(
        front_kernel,
        [(cells, BF16)],
        [
            spread,
            pltpu.VMEM(cells, BF16),
            pltpu.VMEM((9 * channels, channels), BF16),
            pltpu.VMEM((3 * channels, channels), BF16),
            pltpu.VMEM((6 * channels, channels), BF16),
            pltpu.VMEM((channels, 9 * channels), F32),
            pltpu.VMEM((channels, 3 * channels), F32),
            pltpu.VMEM((12 * channels, channels), BF16),
            pltpu.SemaphoreType.DMA((15,)),
        ],
        "front",
        in_hbm=2,
        outs_hbm=[(cells, BF16)] + [(pair, BF16)] * 2 + [(line, BF16)] * 2 + [((12 * channels, channels), BF16)],
    )(latent, row_b, row_a, cot_forward, cot_reverse, cots_b, cots_a, w_space, w_time)

    near, far = len(NEAR[0]), len(FAR[0])
    positions = frame_count * height * width_cells * lax.axis_size("tm") * lax.axis_size("tile")
    shares = sum_to_all(exchange(partial.reshape(near, -1, channels), NEAR), far)
    act_b = swapped(act_b, "tm", 1)
    act_a = swapped(act_a, "tm", 0)
    shares = exchange(shares, FAR)
    out_forward, out_reverse = vmem_call(outs_kernel, [(cells, BF16), (cells, BF16)], (), "outs", cost=pl.CostEstimate(flops=8000000000, bytes_accessed=6 << 20, transcendentals=0))(
        latent, act, act_b, act_a, w_time
    )
    shares, out_forward, out_reverse = lax.optimization_barrier((shares, out_forward, out_reverse))
    shares = sum_to_all(shares, near, 1.0 / math.sqrt(positions))
    shares, gp_b, gp_a = lax.optimization_barrier((shares, gp_b, gp_a))
    whole = exchange(shares, NEAR)
    gp_b = swapped(gp_b, "tile", 1)
    gp_a = swapped(gp_a, "tile", 0)
    (grad_input,) = vmem_call(
        input_kernel, [(cells, BF16)], [spread, pltpu.VMEM((9 * channels, channels), BF16)], "grad_input"
    )(gp, gp_b, gp_a, cot_forward, cot_reverse, w_space)
    grad_spatial, grad_temporal = vmem_call(
        widen_kernel, [((9 * channels, channels), F32), ((3 * channels, channels), F32)], (), "widen"
    )(whole)
    grad_spatial = grad_spatial.reshape(3, 3, channels, channels)
    grad_temporal = grad_temporal.reshape(3, channels, channels)
    return (out_forward, out_reverse, grad_input, grad_spatial, grad_temporal)


def solution(mesh):
    cells = P("tm", "tile", None, None)
    return jax.shard_map(
        body,
        mesh=mesh,
        in_specs=(cells, cells, cells, P(), P()),
        out_specs=(cells, cells, cells, P(), P()),
        check_vma=False,
    )
```

```python
import functools
import math

import jax
import jax.numpy as jnp
from jax import lax
from jax.experimental import pallas as pl
from jax.experimental.pallas import tpu as pltpu
from jax.sharding import PartitionSpec as P

BOTH = ("tm", "tile")
F32 = jnp.float32
BF16 = jnp.bfloat16


def groups(bits):
    rest = [b for b in range(9) if b not in bits]
    out = []
    for r in range(1 << len(rest)):
        base = sum(((r >> i) & 1) << b for i, b in enumerate(rest))
        members = []
        for k in range(1 << len(bits)):
            members.append(base + sum(((k >> i) & 1) << b for i, b in enumerate(reversed(bits))))
        out.append(members)
    return out


NEAR = groups([8, 5, 4, 3, 0])
FAR = groups([7, 6, 2, 1])


def exchange(pieces, members):
    return lax.all_to_all(pieces, BOTH, 0, 0, tiled=True, axis_index_groups=members)


def swapped(value, axis, phase):
    count = lax.axis_size(axis)
    pairs = []
    for i in range(phase, count - 1, 2):
        pairs += [(i, i + 1), (i + 1, i)]
    return lax.ppermute(value, axis, pairs)


def is_even(axis):
    return lax.rem(lax.axis_index(axis), 2) == 0


def vmem_call(kernel, outs, scratch=(), name=None, in_hbm=0, outs_hbm=(), pin=False, cost=None):
    space = pl.BlockSpec(memory_space=pltpu.VMEM)

    def call(*args):
        return pl.pallas_call(
            kernel,
            out_shape=tuple((pltpu.VMEM if pin else jax.ShapeDtypeStruct)(s, t) for s, t in outs)
            + tuple(pltpu.HBM(s, t) for s, t in outs_hbm),
            in_specs=[space] * (len(args) - in_hbm)
            + [pl.BlockSpec(memory_space=pltpu.HBM)] * in_hbm,
            out_specs=tuple(space for _ in outs)
            + tuple(pl.BlockSpec(memory_space=pltpu.HBM) for _ in outs_hbm),
            scratch_shapes=list(scratch),
            compiler_params=pltpu.CompilerParams(vmem_limit_bytes=20 << 20),
            name=name,
            cost_estimate=cost,
        )(*args[: len(args) - in_hbm], *(held(a) for a in args[len(args) - in_hbm :]))

    return call


def held(value):
    return pltpu.with_memory_space_constraint(value, pltpu.HBM)


def edges_kernel(lat, fwd, rev, cots_a, cots_b, row_a, row_b, sems):
    even = is_even("tm")
    head, tail = fwd.at[pl.ds(0, 2)], rev.at[pl.ds(2, 2)]
    at = jnp.where(is_even("tile"), 3, 0)

    @pl.when(even)
    def _():
        pltpu.make_async_copy(tail, cots_a, sems.at[0]).start()
        pltpu.make_async_copy(head, cots_b, sems.at[1]).start()

    @pl.when(jnp.logical_not(even))
    def _():
        pltpu.make_async_copy(head, cots_a, sems.at[0]).start()
        pltpu.make_async_copy(tail, cots_b, sems.at[1]).start()

    pltpu.make_async_copy(lat.at[:, at], row_a, sems.at[2]).start()
    pltpu.make_async_copy(lat.at[:, 3 - at], row_b, sems.at[3]).start()
    pltpu.make_async_copy(head, cots_a, sems.at[0]).wait()
    pltpu.make_async_copy(tail, cots_b, sems.at[1]).wait()
    pltpu.make_async_copy(lat.at[:, at], row_a, sems.at[2]).wait()
    pltpu.make_async_copy(lat.at[:, 3 - at], row_b, sems.at[3]).wait()


def edges(lat, fwd, rev):
    frames, rows, width, channels = lat.shape
    line = (frames, width, channels)
    pair = (2, rows, width, channels)
    anywhere = pl.BlockSpec(memory_space=pl.ANY)
    return pl.pallas_call(
        edges_kernel,
        out_shape=tuple(jax.ShapeDtypeStruct(s, BF16) for s in (pair, pair, line, line)),
        in_specs=[anywhere] * 3,
        out_specs=(pl.BlockSpec(memory_space=pltpu.VMEM),) * 4,
        scratch_shapes=[pltpu.SemaphoreType.DMA((4,))],
        name="edges",
    )(held(lat), held(fwd), held(rev))


def beside(row):
    width = row.shape[0]
    wide = row.astype(F32)
    place = lax.broadcasted_iota(jnp.int32, wide.shape, 0)
    left = jnp.where(place == 0, 0.0, pltpu.roll(wide, 1, 0))
    right = jnp.where(place == width - 1, 0.0, pltpu.roll(wide, width - 1, 0))
    return jnp.concatenate([left.astype(BF16), row, right.astype(BF16)], axis=1)


def windows(rows):
    return jnp.concatenate([rows[i : i + 4].reshape(640, 384) for i in range(3)], axis=1)


def spread_frame(own, got_a, got_b, even, out, frame):
    one, two = got_a[frame], got_b[frame]
    out[frame, 0] = beside(jnp.where(even, two, one))
    for r in range(4):
        out[frame, r + 1] = beside(own[frame, r])
    out[frame, 5] = beside(jnp.where(even, one, two))


def transposed(block):
    return jnp.transpose(block.astype(F32))


def prep_kernel(
    lat, fwd, rev, w_space_at, w_time_at, spread, pre, grad_act, w_space, back, w_time, sems
):
    loads = [
        pltpu.make_async_copy(w_time_at, w_time, sems.at[0]),
        pltpu.make_async_copy(w_space_at, w_space, sems.at[1]),
    ]
    for c in loads:
        c.start()
    for f in range(4):
        for r in range(4):
            spread[f, r] = beside(lat[f, r])
    for c in loads:
        c.wait()
    for k in range(3):
        turned = transposed(w_time[k * 128 : (k + 1) * 128, :]).astype(BF16)
        back[k * 128 : (k + 1) * 128, :] = turned
        back[384 + k * 128 : 384 + (k + 1) * 128, :] = turned
    outside = jnp.zeros((1, 160, 384), BF16)
    for f in range(4):
        patches = windows(jnp.concatenate([outside, spread[f], outside], axis=0))
        rows = slice(f * 640, f * 640 + 640)
        pre[rows, :] = jnp.dot(patches, w_space[...], preferred_element_type=F32)
        ahead, behind = min(3, 4 - f), min(3, f + 1)
        cots = [fwd[f + k] for k in range(ahead)] + [rev[f - k] for k in range(behind)]
        cots = jnp.concatenate([c.reshape(640, 128) for c in cots], axis=1)
        weights = jnp.concatenate([back[: ahead * 128, :], back[384 : 384 + behind * 128, :]], axis=0)
        grad_act[rows, :] = jnp.dot(cots, weights, preferred_element_type=F32)


def front_kernel(
    spread, pre_own, grad_own, w_space, back, cots_b, cots_a, row_b, row_a, fwd, rev,
    act_out, gp_out, act_a, act_b, gp_a, gp_b, partial,
    gp, acc_space, acc_time, summed, sems,
):
    even_tm, even_tile = is_even("tm"), is_even("tile")
    stores = []
    for f in range(4):
        top = beside(jnp.where(even_tile, row_b[f], row_a[f]))
        bottom = beside(jnp.where(even_tile, row_a[f], row_b[f]))
        patches = windows(jnp.concatenate([top[None], spread[f], bottom[None]], axis=0))
        at = f * 640
        pre = jnp.concatenate(
            [
                pre_own[at : at + 160, :]
                + jnp.dot(top, w_space[:384, :], preferred_element_type=F32),
                pre_own[at + 160 : at + 480, :],
                pre_own[at + 480 : at + 640, :]
                + jnp.dot(bottom, w_space[768:, :], preferred_element_type=F32),
            ],
            axis=0,
        )
        sig = 0.5 + 0.5 * jnp.tanh(0.5 * pre)
        act32 = pre * sig
        act = act32.astype(BF16)
        act_out[f] = act.reshape(4, 160, 128)
        cots, sent, weights = [], [], []
        for k in range(3):
            if f + k < 4:
                cots.append(fwd[f + k].reshape(640, 128))
            else:
                at = f + k - 4
                sent.append(jnp.where(even_tm, cots_a[at], cots_b[at]).reshape(640, 128))
                weights.append(back[k * 128 : (k + 1) * 128, :])
                cots.append(sent[-1])
        for k in range(3):
            if f >= k:
                cots.append(rev[f - k].reshape(640, 128))
            else:
                at = f - k + 2
                sent.append(jnp.where(even_tm, cots_b[at], cots_a[at]).reshape(640, 128))
                weights.append(back[k * 128 : (k + 1) * 128, :])
                cots.append(sent[-1])
        cots = jnp.concatenate(cots, axis=1)
        grad_act = grad_own[f * 640 : f * 640 + 640, :] + jnp.dot(
            jnp.concatenate(sent, axis=1),
            jnp.concatenate(weights, axis=0),
            preferred_element_type=F32,
        )
        grad = (grad_act * (sig + act32 * (1.0 - sig))).astype(BF16)
        gp[f] = grad.reshape(4, 160, 128)
        gp_copy = pltpu.make_async_copy(gp.at[f], gp_out.at[f], sems.at[7 + f])
        gp_copy.start()
        stores.append(gp_copy)
        turn = transposed(grad).astype(BF16)
        more = jnp.dot(turn, patches, preferred_element_type=F32)
        turn = transposed(act).astype(BF16)
        more_time = jnp.dot(turn, cots, preferred_element_type=F32)
        more_time = more_time[:, :384] + more_time[:, 384:]
        if f == 0:
            acc_space[...] = more
            acc_time[...] = more_time
        else:
            acc_space[...] += more
            acc_time[...] += more_time
    at_frame, at_row = jnp.where(even_tm, 2, 0), jnp.where(even_tile, 3, 0)
    edge_stores = [
        pltpu.make_async_copy(act_out.at[pl.ds(at_frame, 2)], act_a, sems.at[2]),
        pltpu.make_async_copy(act_out.at[pl.ds(2 - at_frame, 2)], act_b, sems.at[3]),
        pltpu.make_async_copy(gp.at[:, at_row], gp_a, sems.at[4]),
        pltpu.make_async_copy(gp.at[:, 3 - at_row], gp_b, sems.at[5]),
    ]
    for c in edge_stores:
        c.start()
    stores += edge_stores
    for k in range(3):
        summed[(9 + k) * 128 : (10 + k) * 128, :] = acc_time[:, k * 128 : (k + 1) * 128].astype(BF16)
    for part in (3, 0, 1, 2):
        if part < 3:
            for k in range(part * 3, part * 3 + 3):
                summed[k * 128 : (k + 1) * 128, :] = jnp.transpose(
                    acc_space[:, k * 128 : (k + 1) * 128]
                ).astype(BF16)
        rows = pl.ds(part * 384, 384)
        stores.append(pltpu.make_async_copy(summed.at[rows], partial.at[rows], sems.at[11 + part]))
        stores[-1].start()
    for c in stores:
        c.wait()


def sum_kernel(scale, pieces, out):
    total = pieces[0].astype(F32)
    for k in range(1, pieces.shape[0]):
        total += pieces[k].astype(F32)
    total = (total * scale).astype(BF16)
    for k in range(out.shape[0]):
        out[k] = total


def sum_to_all(pieces, count, scale=1.0):
    (copies,) = vmem_call(
        functools.partial(sum_kernel, scale), [((count, *pieces.shape[1:]), BF16)], (), "share"
    )(pieces)
    return copies


def widen_kernel(pieces, space, time):
    rows = pieces.shape[1]
    for k in range(pieces.shape[0]):
        at = k * rows
        if at < space.shape[0]:
            space[at : at + rows, :] = pieces[k].astype(F32)
        else:
            at -= space.shape[0]
            time[at : at + rows, :] = pieces[k].astype(F32)


def outs_kernel(lat, act, got_b, got_a, w_time, out_f, out_r):
    even = is_even("tm")

    def frame(t):
        if t < 0:
            return jnp.where(even, got_b[t + 2], got_a[t + 2])
        if t < 4:
            return act[t]
        return jnp.where(even, got_a[t - 4], got_b[t - 4])

    for t in range(4):
        residual = lat[t].reshape(640, 128).astype(F32)
        for sign, out in ((-1, out_f), (1, out_r)):
            rows = jnp.concatenate([frame(t + sign * k).reshape(640, 128) for k in range(3)], axis=1)
            total = residual + jnp.dot(rows, w_time[...], preferred_element_type=F32)
            out[t] = total.astype(BF16).reshape(4, 160, 128)


def input_kernel(gp, got_b, got_a, fwd, rev, w_space, out, spread, back):
    even = is_even("tile")
    for i in range(3):
        for j in range(3):
            at = (i * 3 + j) * 128
            back[at : at + 128, :] = transposed(
                w_space[((2 - i) * 3 + 2 - j) * 128 : ((2 - i) * 3 + 3 - j) * 128, :]
            ).astype(BF16)
    for f in range(4):
        spread_frame(gp, got_a, got_b, even, spread, f)
        patches = windows(spread[f])
        total = fwd[f].astype(F32) + rev[f].astype(F32)
        total = total.reshape(640, 128) + jnp.dot(patches, back[...], preferred_element_type=F32)
        out[f] = total.astype(BF16).reshape(4, 160, 128)


def body(latent, cot_forward, cot_reverse, spatial_weight, temporal_weight):
    frame_count, height, width_cells, channels = latent.shape
    cells = latent.shape
    line = (frame_count, width_cells, channels)
    pair = (2, height, width_cells, channels)
    w_space = spatial_weight.reshape(9 * channels, channels)
    w_time = temporal_weight.reshape(3 * channels, channels)
    spread = pltpu.VMEM((frame_count, height + 2, width_cells, 3 * channels), BF16)

    cots_a, cots_b, row_a, row_b = edges(latent, cot_forward, cot_reverse)
    cots_b = swapped(cots_b, "tm", 1)
    cots_a = swapped(cots_a, "tm", 0)
    row_b = swapped(row_b, "tile", 1)
    row_a = swapped(row_a, "tile", 0)
    flat = (frame_count * height * width_cells, channels)
    weights = (9 * channels, channels)
    own = vmem_call(
        prep_kernel,
        [
            ((frame_count, height, width_cells, 3 * channels), BF16),
            (flat, F32), (flat, F32), (weights, BF16), ((6 * channels, channels), BF16),
        ],
        [pltpu.VMEM((3 * channels, channels), BF16), pltpu.SemaphoreType.DMA((2,))],
        "prep",
        in_hbm=2,
        pin=True,

    )(latent, cot_forward, cot_reverse, w_space, w_time)
    act, gp, act_a, act_b, gp_a, gp_b, partial = vmem_call(
        front_kernel,
        [(cells, BF16)],
        [
            pltpu.VMEM(cells, BF16),
            pltpu.VMEM((channels, 9 * channels), F32),
            pltpu.VMEM((channels, 3 * channels), F32),
            pltpu.VMEM((12 * channels, channels), BF16),
            pltpu.SemaphoreType.DMA((15,)),
        ],
        "front",
        outs_hbm=[(cells, BF16)] + [(pair, BF16)] * 2 + [(line, BF16)] * 2 + [((12 * channels, channels), BF16)],
    )(*(pltpu.with_memory_space_constraint(o, pltpu.VMEM) for o in own), cots_b, cots_a, row_b, row_a, cot_forward, cot_reverse)

    near, far = len(NEAR[0]), len(FAR[0])
    positions = frame_count * height * width_cells * lax.axis_size("tm") * lax.axis_size("tile")
    shares = sum_to_all(exchange(partial.reshape(near, -1, channels), NEAR), far)
    act_b = swapped(act_b, "tm", 1)
    act_a = swapped(act_a, "tm", 0)
    out_forward, out_reverse = vmem_call(outs_kernel, [(cells, BF16), (cells, BF16)], (), "outs")(
        latent, act, act_b, act_a, w_time
    )
    gp_b, gp_a, out_forward, out_reverse = lax.optimization_barrier((gp_b, gp_a, out_forward, out_reverse))
    gp_b = swapped(gp_b, "tile", 1)
    gp_a = swapped(gp_a, "tile", 0)
    shares = exchange(shares, FAR)
    shares, gp_b, gp_a = lax.optimization_barrier((shares, gp_b, gp_a))
    shares = sum_to_all(shares, near, 1.0 / math.sqrt(positions))
    whole = exchange(shares, NEAR)
    (grad_input,) = vmem_call(
        input_kernel, [(cells, BF16)], [spread, pltpu.VMEM((9 * channels, channels), BF16)], "grad_input"
    )(gp, gp_b, gp_a, cot_forward, cot_reverse, w_space)
    grad_spatial, grad_temporal = vmem_call(
        widen_kernel, [((9 * channels, channels), F32), ((3 * channels, channels), F32)], (), "widen"
    )(whole)
    grad_spatial = grad_spatial.reshape(3, 3, channels, channels)
    grad_temporal = grad_temporal.reshape(3, channels, channels)
    return (out_forward, out_reverse, grad_input, grad_spatial, grad_temporal)


def solution(mesh):
    cells = P("tm", "tile", None, None)
    return jax.shard_map(
        body,
        mesh=mesh,
        in_specs=(cells, cells, cells, P(), P()),
        out_specs=(cells, cells, cells, P(), P()),
        check_vma=False,
    )
```

```python
import functools
import math

import jax
import jax.numpy as jnp
from jax import lax
from jax.experimental import pallas as pl
from jax.experimental.pallas import tpu as pltpu
from jax.sharding import PartitionSpec as P

BOTH = ("tm", "tile")
F32 = jnp.float32
BF16 = jnp.bfloat16


def groups(bits):
    rest = [b for b in range(9) if b not in bits]
    out = []
    for r in range(1 << len(rest)):
        base = sum(((r >> i) & 1) << b for i, b in enumerate(rest))
        members = []
        for k in range(1 << len(bits)):
            members.append(base + sum(((k >> i) & 1) << b for i, b in enumerate(reversed(bits))))
        out.append(members)
    return out


NEAR = groups([8, 5, 4, 3, 0])
FAR = groups([7, 6, 2, 1])


def exchange(pieces, members):
    return lax.all_to_all(pieces, BOTH, 0, 0, tiled=True, axis_index_groups=members)


def swapped(value, axis, phase):
    count = lax.axis_size(axis)
    pairs = []
    for i in range(phase, count - 1, 2):
        pairs += [(i, i + 1), (i + 1, i)]
    return lax.ppermute(value, axis, pairs)


def is_even(axis):
    return lax.rem(lax.axis_index(axis), 2) == 0


def vmem_call(kernel, outs, scratch=(), name=None, in_hbm=0, outs_hbm=(), pin=False, cost=None):
    space = pl.BlockSpec(memory_space=pltpu.VMEM)

    def call(*args):
        return pl.pallas_call(
            kernel,
            out_shape=tuple((pltpu.VMEM if pin else jax.ShapeDtypeStruct)(s, t) for s, t in outs)
            + tuple(pltpu.HBM(s, t) for s, t in outs_hbm),
            in_specs=[space] * (len(args) - in_hbm)
            + [pl.BlockSpec(memory_space=pltpu.HBM)] * in_hbm,
            out_specs=tuple(space for _ in outs)
            + tuple(pl.BlockSpec(memory_space=pltpu.HBM) for _ in outs_hbm),
            scratch_shapes=list(scratch),
            compiler_params=pltpu.CompilerParams(vmem_limit_bytes=20 << 20),
            name=name,
            cost_estimate=cost,
        )(*args[: len(args) - in_hbm], *(held(a) for a in args[len(args) - in_hbm :]))

    return call


def held(value):
    return pltpu.with_memory_space_constraint(value, pltpu.HBM)


def edges_kernel(lat, fwd, rev, cots_a, cots_b, row_a, row_b, sems):
    even = is_even("tm")
    head, tail = fwd.at[pl.ds(0, 2)], rev.at[pl.ds(2, 2)]
    at = jnp.where(is_even("tile"), 3, 0)

    @pl.when(even)
    def _():
        pltpu.make_async_copy(tail, cots_a, sems.at[0]).start()
        pltpu.make_async_copy(head, cots_b, sems.at[1]).start()

    @pl.when(jnp.logical_not(even))
    def _():
        pltpu.make_async_copy(head, cots_a, sems.at[0]).start()
        pltpu.make_async_copy(tail, cots_b, sems.at[1]).start()

    pltpu.make_async_copy(lat.at[:, at], row_a, sems.at[2]).start()
    pltpu.make_async_copy(lat.at[:, 3 - at], row_b, sems.at[3]).start()
    pltpu.make_async_copy(head, cots_a, sems.at[0]).wait()
    pltpu.make_async_copy(tail, cots_b, sems.at[1]).wait()
    pltpu.make_async_copy(lat.at[:, at], row_a, sems.at[2]).wait()
    pltpu.make_async_copy(lat.at[:, 3 - at], row_b, sems.at[3]).wait()


def edges(lat, fwd, rev):
    frames, rows, width, channels = lat.shape
    line = (frames, width, channels)
    pair = (2, rows, width, channels)
    return vmem_call(
        edges_kernel,
        [(pair, BF16), (pair, BF16), (line, BF16), (line, BF16)],
        [pltpu.SemaphoreType.DMA((4,))],
        "edges",
        in_hbm=3,
        pin=True,
    )(lat, fwd, rev)


def beside(row):
    width = row.shape[0]
    wide = row.astype(F32)
    place = lax.broadcasted_iota(jnp.int32, wide.shape, 0)
    left = jnp.where(place == 0, 0.0, pltpu.roll(wide, 1, 0))
    right = jnp.where(place == width - 1, 0.0, pltpu.roll(wide, width - 1, 0))
    return jnp.concatenate([left.astype(BF16), row, right.astype(BF16)], axis=1)


def windows(rows):
    return jnp.concatenate([rows[i : i + 4].reshape(640, 384) for i in range(3)], axis=1)


def spread_frame(own, got_a, got_b, even, out, frame):
    one, two = got_a[frame], got_b[frame]
    out[frame, 0] = beside(jnp.where(even, two, one))
    for r in range(4):
        out[frame, r + 1] = beside(own[frame, r])
    out[frame, 5] = beside(jnp.where(even, one, two))


def transposed(block):
    return jnp.transpose(block.astype(F32))


def prep_kernel(
    lat, fwd, rev, w_space_at, w_time_at, spread, pre, grad_act, w_space, back, w_time, sems
):
    loads = [
        pltpu.make_async_copy(w_time_at, w_time, sems.at[0]),
        pltpu.make_async_copy(w_space_at, w_space, sems.at[1]),
    ]
    for c in loads:
        c.start()
    for f in range(4):
        for r in range(4):
            spread[f, r] = beside(lat[f, r])
    for c in loads:
        c.wait()
    for k in range(3):
        turned = transposed(w_time[k * 128 : (k + 1) * 128, :]).astype(BF16)
        back[k * 128 : (k + 1) * 128, :] = turned
        back[384 + k * 128 : 384 + (k + 1) * 128, :] = turned
    outside = jnp.zeros((1, 160, 384), BF16)
    for f in range(4):
        patches = windows(jnp.concatenate([outside, spread[f], outside], axis=0))
        rows = slice(f * 640, f * 640 + 640)
        pre[rows, :] = jnp.dot(patches, w_space[...], preferred_element_type=F32)
        ahead, behind = min(3, 4 - f), min(3, f + 1)
        cots = [fwd[f + k] for k in range(ahead)] + [rev[f - k] for k in range(behind)]
        cots = jnp.concatenate([c.reshape(640, 128) for c in cots], axis=1)
        weights = jnp.concatenate([back[: ahead * 128, :], back[384 : 384 + behind * 128, :]], axis=0)
        grad_act[rows, :] = jnp.dot(cots, weights, preferred_element_type=F32)


def front_kernel(
    spread, pre_own, grad_own, w_space, back, cots_b, cots_a, row_b, row_a, fwd, rev,
    act_out, gp_out, act_a, act_b, gp_a, gp_b, partial,
    gp, acc_space, acc_time, summed, sems,
):
    even_tm, even_tile = is_even("tm"), is_even("tile")
    stores = []
    for f in range(4):
        top = beside(jnp.where(even_tile, row_b[f], row_a[f]))
        bottom = beside(jnp.where(even_tile, row_a[f], row_b[f]))
        patches = windows(jnp.concatenate([top[None], spread[f], bottom[None]], axis=0))
        at = f * 640
        pre = jnp.concatenate(
            [
                pre_own[at : at + 160, :]
                + jnp.dot(top, w_space[:384, :], preferred_element_type=F32),
                pre_own[at + 160 : at + 480, :],
                pre_own[at + 480 : at + 640, :]
                + jnp.dot(bottom, w_space[768:, :], preferred_element_type=F32),
            ],
            axis=0,
        )
        sig = 0.5 + 0.5 * jnp.tanh(0.5 * pre)
        act32 = pre * sig
        act = act32.astype(BF16)
        act_out[f] = act.reshape(4, 160, 128)
        cots, sent, weights = [], [], []
        for k in range(3):
            if f + k < 4:
                cots.append(fwd[f + k].reshape(640, 128))
            else:
                at = f + k - 4
                sent.append(jnp.where(even_tm, cots_a[at], cots_b[at]).reshape(640, 128))
                weights.append(back[k * 128 : (k + 1) * 128, :])
                cots.append(sent[-1])
        for k in range(3):
            if f >= k:
                cots.append(rev[f - k].reshape(640, 128))
            else:
                at = f - k + 2
                sent.append(jnp.where(even_tm, cots_b[at], cots_a[at]).reshape(640, 128))
                weights.append(back[k * 128 : (k + 1) * 128, :])
                cots.append(sent[-1])
        cots = jnp.concatenate(cots, axis=1)
        grad_act = grad_own[f * 640 : f * 640 + 640, :] + jnp.dot(
            jnp.concatenate(sent, axis=1),
            jnp.concatenate(weights, axis=0),
            preferred_element_type=F32,
        )
        grad = (grad_act * (sig + act32 * (1.0 - sig))).astype(BF16)
        gp[f] = grad.reshape(4, 160, 128)
        gp_copy = pltpu.make_async_copy(gp.at[f], gp_out.at[f], sems.at[7 + f])
        gp_copy.start()
        stores.append(gp_copy)
        turn = transposed(grad).astype(BF16)
        more = jnp.dot(turn, patches, preferred_element_type=F32)
        turn = transposed(act).astype(BF16)
        more_time = jnp.dot(turn, cots, preferred_element_type=F32)
        more_time = more_time[:, :384] + more_time[:, 384:]
        if f == 0:
            acc_space[...] = more
            acc_time[...] = more_time
        else:
            acc_space[...] += more
            acc_time[...] += more_time
    at_frame, at_row = jnp.where(even_tm, 2, 0), jnp.where(even_tile, 3, 0)
    edge_stores = [
        pltpu.make_async_copy(act_out.at[pl.ds(at_frame, 2)], act_a, sems.at[2]),
        pltpu.make_async_copy(act_out.at[pl.ds(2 - at_frame, 2)], act_b, sems.at[3]),
        pltpu.make_async_copy(gp.at[:, at_row], gp_a, sems.at[4]),
        pltpu.make_async_copy(gp.at[:, 3 - at_row], gp_b, sems.at[5]),
    ]
    for c in edge_stores:
        c.start()
    stores += edge_stores
    for k in range(3):
        summed[(9 + k) * 128 : (10 + k) * 128, :] = acc_time[:, k * 128 : (k + 1) * 128].astype(BF16)
    for part in (3, 0, 1, 2):
        if part < 3:
            for k in range(part * 3, part * 3 + 3):
                summed[k * 128 : (k + 1) * 128, :] = jnp.transpose(
                    acc_space[:, k * 128 : (k + 1) * 128]
                ).astype(BF16)
        rows = pl.ds(part * 384, 384)
        stores.append(pltpu.make_async_copy(summed.at[rows], partial.at[rows], sems.at[11 + part]))
        stores[-1].start()
    for c in stores:
        c.wait()


def sum_kernel(scale, pieces, out):
    total = pieces[0].astype(F32)
    for k in range(1, pieces.shape[0]):
        total += pieces[k].astype(F32)
    total = (total * scale).astype(BF16)
    for k in range(out.shape[0]):
        out[k] = total


def sum_to_all(pieces, count, scale=1.0):
    (copies,) = vmem_call(
        functools.partial(sum_kernel, scale), [((count, *pieces.shape[1:]), BF16)], (), "share"
    )(pieces)
    return copies


def widen_kernel(pieces, space, time):
    rows = pieces.shape[1]
    for k in range(pieces.shape[0]):
        at = k * rows
        if at < space.shape[0]:
            space[at : at + rows, :] = pieces[k].astype(F32)
        else:
            at -= space.shape[0]
            time[at : at + rows, :] = pieces[k].astype(F32)


def outs_kernel(lat, act, got_b, got_a, w_time, out_f, out_r):
    even = is_even("tm")

    def frame(t):
        if t < 0:
            return jnp.where(even, got_b[t + 2], got_a[t + 2])
        if t < 4:
            return act[t]
        return jnp.where(even, got_a[t - 4], got_b[t - 4])

    for t in range(4):
        residual = lat[t].reshape(640, 128).astype(F32)
        for sign, out in ((-1, out_f), (1, out_r)):
            rows = jnp.concatenate([frame(t + sign * k).reshape(640, 128) for k in range(3)], axis=1)
            total = residual + jnp.dot(rows, w_time[...], preferred_element_type=F32)
            out[t] = total.astype(BF16).reshape(4, 160, 128)


def input_kernel(gp, got_b, got_a, fwd, rev, w_space, out, spread, back):
    even = is_even("tile")
    for i in range(3):
        for j in range(3):
            at = (i * 3 + j) * 128
            back[at : at + 128, :] = transposed(
                w_space[((2 - i) * 3 + 2 - j) * 128 : ((2 - i) * 3 + 3 - j) * 128, :]
            ).astype(BF16)
    for f in range(4):
        spread_frame(gp, got_a, got_b, even, spread, f)
        patches = windows(spread[f])
        total = fwd[f].astype(F32) + rev[f].astype(F32)
        total = total.reshape(640, 128) + jnp.dot(patches, back[...], preferred_element_type=F32)
        out[f] = total.astype(BF16).reshape(4, 160, 128)


def body(latent, cot_forward, cot_reverse, spatial_weight, temporal_weight):
    frame_count, height, width_cells, channels = latent.shape
    cells = latent.shape
    line = (frame_count, width_cells, channels)
    pair = (2, height, width_cells, channels)
    w_space = spatial_weight.reshape(9 * channels, channels)
    w_time = temporal_weight.reshape(3 * channels, channels)
    spread = pltpu.VMEM((frame_count, height + 2, width_cells, 3 * channels), BF16)

    cots_a, cots_b, row_a, row_b = edges(latent, cot_forward, cot_reverse)
    cots_b = swapped(cots_b, "tm", 1)
    cots_a = swapped(cots_a, "tm", 0)
    row_b = swapped(row_b, "tile", 1)
    row_a = swapped(row_a, "tile", 0)
    flat = (frame_count * height * width_cells, channels)
    weights = (9 * channels, channels)
    own = vmem_call(
        prep_kernel,
        [
            ((frame_count, height, width_cells, 3 * channels), BF16),
            (flat, F32), (flat, F32), (weights, BF16), ((6 * channels, channels), BF16),
        ],
        [pltpu.VMEM((3 * channels, channels), BF16), pltpu.SemaphoreType.DMA((2,))],
        "prep",
        in_hbm=2,
        pin=True,

    )(latent, cot_forward, cot_reverse, w_space, w_time)
    act, gp, act_a, act_b, gp_a, gp_b, partial = vmem_call(
        front_kernel,
        [(cells, BF16)],
        [
            pltpu.VMEM(cells, BF16),
            pltpu.VMEM((channels, 9 * channels), F32),
            pltpu.VMEM((channels, 3 * channels), F32),
            pltpu.VMEM((12 * channels, channels), BF16),
            pltpu.SemaphoreType.DMA((15,)),
        ],
        "front",
        outs_hbm=[(cells, BF16)] + [(pair, BF16)] * 2 + [(line, BF16)] * 2 + [((12 * channels, channels), BF16)],
    )(*(pltpu.with_memory_space_constraint(o, pltpu.VMEM) for o in own), cots_b, cots_a, row_b, row_a, cot_forward, cot_reverse)

    near, far = len(NEAR[0]), len(FAR[0])
    positions = frame_count * height * width_cells * lax.axis_size("tm") * lax.axis_size("tile")
    shares = sum_to_all(exchange(partial.reshape(near, -1, channels), NEAR), far)
    act_b = swapped(act_b, "tm", 1)
    act_a = swapped(act_a, "tm", 0)
    out_forward, out_reverse = vmem_call(outs_kernel, [(cells, BF16), (cells, BF16)], (), "outs")(
        latent, act, act_b, act_a, w_time
    )
    gp_b, gp_a, out_forward, out_reverse = lax.optimization_barrier((gp_b, gp_a, out_forward, out_reverse))
    gp_b = swapped(gp_b, "tile", 1)
    gp_a = swapped(gp_a, "tile", 0)
    shares = exchange(shares, FAR)
    shares, gp_b, gp_a = lax.optimization_barrier((shares, gp_b, gp_a))
    shares = sum_to_all(shares, near, 1.0 / math.sqrt(positions))
    whole = exchange(shares, NEAR)
    (grad_input,) = vmem_call(
        input_kernel, [(cells, BF16)], [spread, pltpu.VMEM((9 * channels, channels), BF16)], "grad_input"
    )(gp, gp_b, gp_a, cot_forward, cot_reverse, w_space)
    grad_spatial, grad_temporal = vmem_call(
        widen_kernel, [((9 * channels, channels), F32), ((3 * channels, channels), F32)], (), "widen"
    )(whole)
    grad_spatial = grad_spatial.reshape(3, 3, channels, channels)
    grad_temporal = grad_temporal.reshape(3, channels, channels)
    return (out_forward, out_reverse, grad_input, grad_spatial, grad_temporal)


def solution(mesh):
    cells = P("tm", "tile", None, None)
    return jax.shard_map(
        body,
        mesh=mesh,
        in_specs=(cells, cells, cells, P(), P()),
        out_specs=(cells, cells, cells, P(), P()),
        check_vma=False,
    )
```
